32 devices in a mesh: stream: 8 (over z, x), span: 4 (over y, core).
Axes of the slice: x: 2, y: 2, z: 4, core: 2. Of those that a mesh axis runs over, the one named last changes fastest.
Arguments:
- checkpoint: float32 [5, 192, 8, 512], P(None, None, 'stream', 'span'), may hold values from -4.8 to 4.8
- adjoint: float32 [5, 192, 8, 512], P(None, None, 'stream', 'span'), may hold values from -6 to 6
- line_inverse: bfloat16 [8, 3, 320, 320], P('stream'), may hold values from -0.3125 to 0.3125
- row_source: int32 [768], replicated, may hold values from 0 to 767, as said below
Outputs:
- adjoint_start: float32 [5, 192, 8, 512], P(None, None, 'stream', 'span')
The draws below stay inside these ranges and needn't reach their ends.
Inputs may be any that keep to these rules, and one draw needn't show every extreme that they name: `row_source`: every rotor outlet row is taken by exactly one stator inlet row, and each stator span tile takes exactly 48 rows from each rotor span tile.
All inputs are finite; a program needn't handle non-finite values.
Results may differ from the reference program's by a relative error of at most 0.0029.
Values sent between devices are 32-bit elements; how exact they have to be, the bound alone decides.
No kernel may reach another device: no remote copies, remote signals or barrier semaphores. Data moves between devices by JAX's collectives and lax.ppermute only.
A program may use at most 64 MiB of HBM per device.

```python
import jax
import jax.numpy as jnp
from jax import lax

NC = 5
NL = 192
LB = 64
CP = 128
NB = 3
NS = 8
NP = 512
SPLIT = 4
IROWS = 768
CAP = 48
N_SPAN = 4


def draw_row_source(key, part):
    key_rows, key_mix = jax.random.split(jax.random.fold_in(key, 7))
    first_keys = jax.random.split(key_rows, N_SPAN)
    row_order = jax.vmap(lambda subkey: jax.random.permutation(subkey, NL))(first_keys).astype(jnp.int32)
    grouped = row_order.reshape(N_SPAN, N_SPAN, CAP)
    global_rows = grouped + (jnp.arange(N_SPAN, dtype=jnp.int32) * NL)[:, None, None]
    per_dest = jnp.transpose(global_rows, (1, 0, 2)).reshape(N_SPAN, NL)
    second_keys = jax.random.split(key_mix, N_SPAN)
    shuffle = jax.vmap(lambda subkey: jax.random.permutation(subkey, NL))(second_keys).astype(jnp.int32)
    shuffled_rows = jnp.take_along_axis(per_dest, shuffle, axis=1)
    return shuffled_rows.reshape(IROWS).astype(jnp.int32)


def shard_levels(key, shape, pieces, smallest, top_value):
    loudness = 1.0
    for axis_at, blocks in pieces:
        draws = jax.random.uniform(jax.random.fold_in(jax.random.fold_in(key, 6), axis_at), (blocks,), jnp.float32, smallest / len(pieces), top_value / len(pieces))
        loudness = loudness * jnp.repeat(jnp.exp(draws), shape[axis_at] // blocks).reshape((-1,) + (1,) * (len(shape) - 1 - axis_at))
    return loudness


def centred(own_key, extent, deviation, most, cuts=(), held_as=jnp.bfloat16):
    factor_of = shard_levels(own_key, extent, cuts, -0.22, 0.18) if cuts else 1.0
    values = jax.random.normal(own_key, extent, jnp.float32) * deviation * factor_of
    return jnp.minimum(jnp.maximum(values, -most), most).astype(held_as)


def setup_inputs(seed: int = 0) -> dict:
    splits = jax.random.split(jax.random.key(seed), 5)
    return {
        "checkpoint": centred(splits[0], (NC, NL, NS, NP), 0.8, 4.8, ((2, 8), (3, 4)), jnp.float32),
        "adjoint": centred(splits[1], (NC, NL, NS, NP), 1.0, 6.0, ((2, 8), (3, 4)), jnp.float32),
        "line_inverse": centred(splits[2], (NS, NB, NC * LB, NC * LB), (NC * LB) ** -0.5, 0.3125, ((0, 8),)),
        "row_source": draw_row_source(jax.random.fold_in(splits[4], 71), 0),
    }


time_step = 0.5
ADVECTION = (1.0, 0.6, 0.8, 1.2, 0.7)
DISSIPATION = (0.3, 0.25, 0.35, 0.3, 0.4)
SPREADING = (0.4, 0.3, 0.5, 0.35, 0.45)


def per_state(values):
    return jnp.array(values, jnp.float32).reshape(5, 1, 1, 1)


def shift_upstream(field, row_source):
    upstream = jnp.concatenate([jnp.zeros_like(field[:, :, :1]), field[:, :, :-1]], axis=2)
    face_rows = field[:, :, SPLIT - 1].reshape(NC, NL, N_SPAN, CP)
    src_dev = (row_source // NL).reshape(N_SPAN, NL)
    src_row = (row_source % NL).reshape(N_SPAN, NL)
    mapped = face_rows[:, src_row, src_dev, :]
    mapped = jnp.transpose(mapped, (0, 2, 1, 3)).reshape(NC, NL, NP)
    return upstream.at[:, :, SPLIT].set(mapped)


def shift_downstream(field, row_source):
    downstream = jnp.concatenate([field[:, :, 1:], jnp.zeros_like(field[:, :, :1])], axis=2)
    inverse_rows = jnp.zeros((IROWS,), jnp.int32).at[row_source].set(jnp.arange(IROWS, dtype=jnp.int32))
    inverse_rows = inverse_rows.reshape(N_SPAN, NL)
    face_rows = field[:, :, SPLIT].reshape(NC, NL, N_SPAN, CP)
    mapped = face_rows[:, inverse_rows % NL, inverse_rows // NL, :]
    mapped = jnp.transpose(mapped, (0, 2, 1, 3)).reshape(NC, NL, NP)
    return downstream.at[:, :, SPLIT - 1].set(mapped)


def operator(field, row_source, coef_down, coef_up, center, lateral):
    lateral_sum = jnp.roll(field, 1, axis=3) + jnp.roll(field, -1, axis=3) - 2.0 * field
    return (coef_down * shift_downstream(field, row_source) + coef_up * shift_upstream(field, row_source)
            + center * field + lateral * lateral_sum)


def reference(checkpoint, adjoint, line_inverse, row_source):
    advect = per_state(ADVECTION)
    dissip = per_state(DISSIPATION)
    lateral = per_state(SPREADING)
    toward_down = -0.5 * advect + dissip
    toward_up = 0.5 * advect + dissip
    center = -2.0 * dissip
    flux = jnp.tanh(checkpoint)
    advanced = checkpoint + time_step * operator(flux, row_source, toward_down, toward_up, center, lateral)
    tanh_adv = jnp.tanh(advanced)
    section_slope = 2.0 - tanh_adv * tanh_adv
    rounded = lax.optimization_barrier(adjoint.astype(jnp.bfloat16)).astype(jnp.float32)
    blocked = rounded.reshape(NC, NB, LB, NS, NP)
    inverse = line_inverse.astype(jnp.float32).reshape(NS, NB, NC, LB, NC, LB)
    carried = jnp.einsum('sbclem,cblsp->ebmsp', inverse, blocked,
                         precision=lax.Precision.HIGHEST).reshape(NC, NL, NS, NP)
    weighted = section_slope * carried
    tangent = 1.0 - flux * flux
    return weighted + time_step * tangent * operator(weighted, row_source, toward_up, toward_down, center, lateral)
```

```python
import jax
import jax.numpy as jnp
from jax import lax
from jax.experimental import pallas as pl
from jax.experimental.pallas import tpu as pltpu
from jax.sharding import PartitionSpec as P

time_step = 0.5
ADVECTION = (1.0, 0.6, 0.8, 1.2, 0.7)
DISSIPATION = (0.3, 0.25, 0.35, 0.3, 0.4)
SPREADING = (0.4, 0.3, 0.5, 0.35, 0.45)
NC = 5
LANES = 128
HALF = 64
AXES = ("stream", "span")
f32 = jnp.float32
bf16 = jnp.bfloat16


class Plan:
    def __init__(self, mesh, rows, blocks, block_rows):
        self.stream = mesh.shape["stream"]
        self.span = mesh.shape["span"]
        self.rows = rows
        self.blocks = blocks
        self.block_rows = block_rows
        self.pairs = self.stream // 2
        self.inlet = self.stream // 4
        assert self.stream % 4 == 0 and self.inlet % 2 == 0 and self.span % 2 == 0
        self.chips = self.span // 2
        self.capacity = rows // self.span
        self.part = self.capacity // 2
        self.part_pad = -(-self.part // 8) * 8
        self.packed = self.span * self.part_pad
        self.slots = 2 * self.packed
        self.swap_x = self.full({})
        boundaries = [z for z in range(self.pairs - 1) if z + 1 != self.inlet]
        self.swap_z = []
        for parity in (0, 1):
            moves = {}
            for z in boundaries:
                if z % 2 == parity:
                    for x in range(2):
                        for j in range(self.span):
                            a, b = self.at(z, x, j), self.at(z + 1, x, j)
                            moves[a], moves[b] = b, a
            if moves:
                self.swap_z.append(self.full(moves))
        self.swap_face = []
        for turn in range(self.chips):
            moves = {}
            for x in range(2):
                for j in range(self.span):
                    other = ((j // 2 + turn) % self.chips) * 2 + j % 2
                    a, b = self.at(self.inlet - 1, x, j), self.at(self.inlet, x, other)
                    moves[a], moves[b] = b, a
            self.swap_face.append(self.full(moves))
        every = [(z, j) for z in range(self.pairs) for j in range(self.span)]
        self.swap_x = self.full(
            {self.at(z, x, j): self.at(z, 1 - x, j) for z, j in every for x in range(2)}
        )
        moves = {}
        for z, j in every:
            a, b = self.at(z, 1, j), self.at(z, 0, (j + 1) % self.span)
            moves[a], moves[b] = b, a
        self.swap_span = self.full(moves)
        self.swap_core = self.full({})

    def at(self, z, x, j):
        return (2 * z + x) * self.span + j

    def full(self, moves):
        count = self.stream * self.span
        return [(d, moves.get(d, d ^ 1)) for d in range(count)]


def place():
    s = lax.axis_index("stream")
    return s // 2, lax.rem(s, 2), lax.axis_index("span")


def lane_ids(rows):
    return lax.broadcasted_iota(jnp.int32, (rows, LANES), 1)


def split2(values):
    high = values.astype(bf16)
    return high, (values - high.astype(f32)).astype(bf16)


def dot(a, b, dims=((1,), (0,))):
    return lax.dot_general(a, b, (dims, ((), ())), preferred_element_type=f32)


def pack(block, high):
    rows = block.shape[0] // 2
    return jnp.where(
        lane_ids(rows) < HALF,
        pltpu.roll(block[:rows], HALF * high, 1),
        pltpu.roll(block[rows:], HALF * (1 - high), 1),
    )


def unpack(packed, high):
    return jnp.concatenate(
        [pltpu.roll(packed, HALF * high, 1), pltpu.roll(packed, HALF * (1 - high), 1)], axis=0
    )


def pack_kernel(block_ref, out_ref):
    _, x, _ = place()
    for c in range(NC):
        out_ref[c] = pack(block_ref[c], 1 - x)


def slot_kernel(plan, source_ref, put_ref, get_ref):
    rows, span, chips = plan.rows, plan.span, plan.chips
    z, _, j = place()
    source = source_ref[...]
    own_chip, own_core = j // 2, lax.rem(j, 2)

    def order(other, sign):
        core = jnp.where(other % 2 == own_core, 0, 1)
        turn = lax.rem(sign * (other // 2 - own_chip) + chips, chips)
        return ((core * chips + turn) * plan.part_pad).astype(f32)

    before = (
        lax.broadcasted_iota(jnp.int32, (rows, rows), 0)
        < lax.broadcasted_iota(jnp.int32, (rows, rows), 1)
    )
    before = jnp.where(before, 1.0, 0.0).astype(bf16)
    sub = lax.broadcasted_iota(jnp.int32, (rows, rows), 0)
    lane = lax.broadcasted_iota(jnp.int32, (rows, rows), 1)
    arrival = jnp.zeros(source.shape, f32)
    base = jnp.zeros(source.shape, f32)
    for d in range(span):
        here = jnp.where((source >= d * rows) & (source < (d + 1) * rows), 1.0, 0.0)
        arrival += here * dot(here.astype(bf16), before)
        base += here * order(d, -1)
    late = jnp.where(arrival >= plan.part, 1.0, 0.0)
    within = arrival + late * (plan.packed - plan.part)
    own = lax.broadcasted_iota(jnp.int32, source.shape, 0) == j
    stator_row = jnp.sum(jnp.where(own, base + within, 0.0), axis=0, keepdims=True)
    total = jnp.zeros((rows, rows), f32)
    for d in range(span):
        match = source[d : d + 1] - j * rows == sub
        total += jnp.where(match, within[d : d + 1] + order(d, 1), 0.0)
    rotor_col = jnp.sum(total, axis=1, keepdims=True)
    same = sub == lane
    stator_col = jnp.sum(jnp.where(same, stator_row, 0.0), axis=1, keepdims=True)
    rotor_row = jnp.sum(jnp.where(same, rotor_col, 0.0), axis=0, keepdims=True)
    stator = z == plan.inlet
    col = jnp.where(stator, stator_col, rotor_col).astype(jnp.int32)
    row = jnp.where(stator, stator_row, rotor_row).astype(jnp.int32)
    put = lax.broadcasted_iota(jnp.int32, (plan.slots, rows), 0) == row
    get = lax.broadcasted_iota(jnp.int32, (rows, plan.slots), 1) == col
    put_ref[...] = jnp.where(put, 1.0, 0.0).astype(bf16)
    get_ref[...] = jnp.where(get, 1.0, 0.0).astype(bf16)


def carried_kernel(plan, adjoint_ref, inverse_ref, carried_ref, out_ref):
    size = plan.block_rows
    for b in range(plan.blocks):
        rounded = jnp.concatenate(
            [adjoint_ref[c, b * size : (b + 1) * size].astype(bf16) for c in range(NC)], axis=0
        )
        product = dot(inverse_ref[b], rounded, ((0,), (0,)))
        for c in range(NC):
            carried_ref[c, b * size : (b + 1) * size] = product[c * size : (c + 1) * size]
    _, x, _ = place()
    for c in range(NC):
        out_ref[c] = pack(carried_ref[c], 1 - x)


def edge_pick(c, low, value_rows=16):
    row = lax.broadcasted_iota(jnp.int32, (value_rows, LANES), 0)
    lane = lax.broadcasted_iota(jnp.int32, (value_rows, LANES), 1)
    hit = ((row == c) & (lane == low)) | ((row == 8 + c) & (lane == low + HALF))
    return jnp.where(hit, 1.0, 0.0).astype(bf16)


def send_parts(plan, field, put_ref, z_refs, face_ref, span_ref, x_ref):
    z, x, _ = place()
    odd = lax.rem(z, 2)
    rotor = z < plan.inlet
    lane = lane_ids(plan.rows)
    keep = jnp.logical_xor(lane < HALF, rotor)
    put = put_ref[...]
    span_edge = jnp.zeros((16, plan.rows), f32)
    x_edge = jnp.zeros((16, plan.rows), f32)
    for c in range(NC):
        block = field(c)
        for parity, ref in enumerate(z_refs):
            ref[c] = pack(block, 1 - odd if parity == 0 else odd)
        both = jnp.where(keep, block, pltpu.roll(block, HALF, 1))
        moved = dot(put, jnp.concatenate(split2(both), axis=1))
        moved = moved[:, :LANES] + moved[:, LANES:]
        packed = jnp.where(lane_ids(plan.packed) < HALF, moved[: plan.packed], moved[plan.packed :])
        for core in range(2):
            for turn in range(plan.chips):
                at = (core * plan.chips + turn) * plan.part_pad
                face_ref[core, turn, c] = packed[at : at + plan.part_pad]
        high, low = split2(block)
        nt = ((1,), (1,))
        pick_span, pick_x = edge_pick(c, 63 * x), edge_pick(c, 63 * (1 - x))
        span_edge += dot(pick_span, high, nt) + dot(pick_span, low, nt)
        x_edge += dot(pick_x, high, nt) + dot(pick_x, low, nt)
    span_ref[...] = span_edge
    x_ref[...] = x_edge


def stencil(plan, c, block, got, get, coef_down, coef_up):
    z_refs, face_refs, edge_high, edge_low = got
    z, x, _ = place()
    odd = lax.rem(z, 2)
    lane = lane_ids(plan.rows)
    low = lane < HALF
    packed = jnp.concatenate(
        [face_refs[t][core, c] for core in range(2) for t in range(plan.chips)], axis=0
    )
    turned = pltpu.roll(packed, HALF, 1)
    low_p = lane_ids(plan.packed) < HALF
    both = jnp.concatenate(
        [jnp.where(low_p, packed, turned), jnp.where(low_p, turned, packed)], axis=0
    )
    other = dot(get, jnp.concatenate(split2(both), axis=1))
    other = other[:, :LANES] + other[:, LANES:]
    at_face = (z == plan.inlet) | (z == plan.inlet - 1)
    at_end = (z == 0) | (z == plan.pairs - 1)
    if len(z_refs) > 1:
        second = unpack(z_refs[1][c], odd)
        other = jnp.where(at_face, other, jnp.where(at_end, 0.0, second))
    else:
        other = jnp.where(at_face, other, 0.0)
    halo = jnp.where(jnp.logical_xor(low, odd == 1), other, unpack(z_refs[0][c], 1 - odd))
    across = pltpu.roll(block, HALF, 1)
    upstream = jnp.where(low, halo, across)
    downstream = jnp.where(low, across, halo)
    spots = jnp.concatenate([edge_pick(c, 63 * x), edge_pick(c, 63 * (1 - x))], axis=0)
    tn = ((0,), (0,))
    ghost = dot(edge_high, spots, tn) + dot(edge_low, spots, tn)
    cell = jnp.bitwise_and(lane, HALF - 1)
    left = jnp.where(cell == 0, 0.0, pltpu.roll(block, 1, 1))
    right = jnp.where(cell == HALF - 1, 0.0, pltpu.roll(block, LANES - 1, 1))
    lateral_sum = left + right + ghost - 2.0 * block
    return (
        coef_down * downstream
        + coef_up * upstream
        - 2.0 * DISSIPATION[c] * block
        + SPREADING[c] * lateral_sum
    )


def paired(plan, own, arrived, x):
    return jnp.where(jnp.logical_xor(lane_ids(plan.rows) < HALF, x == 1), own, unpack(arrived, 1 - x))


def coefficients(c):
    down = -0.5 * ADVECTION[c] + DISSIPATION[c]
    up = 0.5 * ADVECTION[c] + DISSIPATION[c]
    return down, up


def first_kernel(plan, block_ref, arrived_ref, put_ref, state_ref, flux_ref, *outs):
    _, x, _ = place()

    def field(c):
        state = paired(plan, block_ref[c], arrived_ref[c], x)
        flux = jnp.tanh(state)
        state_ref[c] = state
        flux_ref[c] = flux
        return flux

    count = len(plan.swap_z)
    send_parts(plan, field, put_ref, outs[:count], *outs[count:])


def arrived_parts(plan, refs):
    count = len(plan.swap_z)
    z_refs, refs = refs[:count], refs[count:]
    face_refs, refs = refs[: plan.chips], refs[plan.chips :]
    edges = jnp.concatenate([refs[0][...], refs[1][...]], axis=0)
    return (z_refs, face_refs) + split2(edges), refs[2:]


def second_kernel(plan, state_ref, flux_ref, carried_ref, arrived_ref, put_ref, get_ref, *refs):
    _, x, _ = place()
    got, refs = arrived_parts(plan, refs)
    weighted_ref, refs = refs[0], refs[1:]
    get = get_ref[...]

    def field(c):
        down, up = coefficients(c)
        change = stencil(plan, c, flux_ref[c], got, get, down, up)
        slope = jnp.tanh(state_ref[c] + time_step * change)
        slope = 2.0 - slope * slope
        weighted = slope * paired(plan, carried_ref[c], arrived_ref[c], x)
        weighted_ref[c] = weighted
        return weighted

    count = len(plan.swap_z)
    send_parts(plan, field, put_ref, refs[:count], *refs[count:])


def third_kernel(plan, weighted_ref, flux_ref, get_ref, *refs):
    _, x, _ = place()
    got, refs = arrived_parts(plan, refs)
    result_ref, out_ref = refs
    get = get_ref[...]
    for c in range(NC):
        down, up = coefficients(c)
        weighted, flux = weighted_ref[c], flux_ref[c]
        change = stencil(plan, c, weighted, got, get, up, down)
        result = weighted + time_step * (1.0 - flux * flux) * change
        result_ref[c] = result
        out_ref[c] = pack(result, 1 - x)


def last_kernel(plan, result_ref, arrived_ref, out_ref):
    _, x, _ = place()
    for c in range(NC):
        out_ref[c] = paired(plan, result_ref[c], arrived_ref[c], x)


def call(kernel, outs, *args):
    whole = pl.BlockSpec(memory_space=pltpu.VMEM)
    return pl.pallas_call(
        kernel,
        out_shape=[jax.ShapeDtypeStruct(shape, dtype) for shape, dtype in outs],
        in_specs=[whole] * len(args),
        out_specs=[whole] * len(outs),
        compiler_params=pltpu.CompilerParams(vmem_limit_bytes=32 * 2**20),
    )(*args)


def bind(kernel, plan):
    def bound(*refs):
        kernel(plan, *refs)

    return bound


def exchange(plan, parts):
    count = len(plan.swap_z)
    face, span_edge, x_edge = parts[count:]
    crossed = lax.ppermute(face[1], AXES, plan.swap_core)
    z_got = [lax.ppermute(part, AXES, perm) for part, perm in zip(parts, plan.swap_z)]
    face_got = [
        lax.ppermute(jnp.stack([face[0, t], crossed[t]]), AXES, plan.swap_face[t])
        for t in range(plan.chips)
    ]
    span_got = lax.ppermute(span_edge, AXES, plan.swap_span)
    x_got = lax.ppermute(x_edge, AXES, plan.swap_x)
    return z_got + face_got + [span_got, x_got]


def solution(mesh):
    def local(checkpoint, adjoint, line_inverse, row_source):
        rows = checkpoint.shape[1]
        blocks = line_inverse.shape[1]
        plan = Plan(mesh, rows, blocks, rows // blocks)
        full, half = (NC, rows, LANES), (NC, rows // 2, LANES)
        checkpoint = checkpoint.reshape(full)
        adjoint = adjoint.reshape(full)
        inverse = line_inverse.reshape(line_inverse.shape[1:])
        source = row_source.reshape(plan.span, rows)
        source = jnp.pad(source, ((0, -plan.span % 8), (0, 0)), constant_values=-1)
        parts = (
            [(half, f32)] * len(plan.swap_z)
            + [((2, plan.chips, NC, plan.part_pad, LANES), f32)]
            + [((16, rows), f32)] * 2
        )
        (mine,) = call(pack_kernel, [(half, f32)], checkpoint)
        state_got = lax.ppermute(mine, AXES, plan.swap_x)
        carried, mine = call(
            bind(carried_kernel, plan), [(full, f32), (half, f32)], adjoint, inverse
        )
        carried_got = lax.ppermute(mine, AXES, plan.swap_x)
        put, get = call(
            bind(slot_kernel, plan),
            [((plan.slots, rows), bf16), ((rows, plan.slots), bf16)],
            source,
        )
        state, flux, *sent = call(
            bind(first_kernel, plan), [(full, f32)] * 2 + parts, checkpoint, state_got, put
        )
        got = exchange(plan, sent)
        weighted, *sent = call(
            bind(second_kernel, plan),
            [(full, f32)] + parts,
            *(state, flux, carried, carried_got, put, get),
            *got,
        )
        got = exchange(plan, sent)
        result, mine = call(
            bind(third_kernel, plan), [(full, f32), (half, f32)], weighted, flux, get, *got
        )
        result_got = lax.ppermute(mine, AXES, plan.swap_x)
        (out,) = call(bind(last_kernel, plan), [(full, f32)], result, result_got)
        return out.reshape(NC, rows, 1, LANES)

    return jax.shard_map(
        local,
        mesh=mesh,
        in_specs=(
            P(None, None, "stream", "span"),
            P(None, None, "stream", "span"),
            P("stream", None, None, None),
            P(),
        ),
        out_specs=P(None, None, "stream", "span"),
        check_vma=False,
    )
```

```python
import jax
import jax.numpy as jnp
from jax import lax
from jax.experimental import pallas as pl
from jax.experimental.pallas import tpu as pltpu
from jax.sharding import PartitionSpec as P

time_step = 0.5
ADVECTION = (1.0, 0.6, 0.8, 1.2, 0.7)
DISSIPATION = (0.3, 0.25, 0.35, 0.3, 0.4)
SPREADING = (0.4, 0.3, 0.5, 0.35, 0.45)
NC = 5
LANES = 128
HALF = 64
AXES = ("stream", "span")
f32 = jnp.float32
bf16 = jnp.bfloat16
GHOST_FLOPS = 10**10


class Plan:
    def __init__(self, mesh, rows, blocks):
        self.stream = mesh.shape["stream"]
        self.span = mesh.shape["span"]
        self.rows = rows
        self.blocks = blocks
        self.block_rows = rows // blocks
        self.pairs = self.stream // 2
        self.inlet = self.stream // 4
        assert self.stream % 4 == 0 and self.inlet % 2 == 0 and self.span % 2 == 0
        self.chips = self.span // 2
        self.capacity = rows // self.span
        self.part = self.capacity // 2
        self.part_pad = -(-self.part // 8) * 8
        self.packed = self.span * self.part_pad
        self.slots = 2 * self.packed
        self.edge_rows = 8 * -(-rows // LANES)
        zs, js = range(self.pairs), range(self.span)
        self.swap_core = self.full({})
        self.swap_x = self.full(
            {self.at(z, x, j): self.at(z, 1 - x, j) for z in zs for j in js for x in range(2)}
        )
        self.swap_z = []
        for parity in (0, 1):
            moves = {}
            for z in zs[:-1]:
                if z % 2 == parity and z + 1 != self.inlet:
                    for x in range(2):
                        for j in js:
                            self.trade(moves, self.at(z, x, j), self.at(z + 1, x, j))
            if moves:
                self.swap_z.append(self.full(moves))
        self.swap_face, self.straight, self.diag = [], [], []
        for turn in range(self.chips):
            face, straight, diag = {}, {}, {}
            for j in js:
                for z in zs[:-1]:
                    up = down = j
                    if z + 1 == self.inlet:
                        up = (j // 2 + turn) % self.chips * 2 + j % 2
                        down = (j // 2 - turn) % self.chips * 2 + j % 2
                        for x in range(2):
                            self.trade(face, self.at(z, x, j), self.at(z + 1, x, up))
                    straight[self.at(z, 0, j)] = self.at(z + 1, 0, up)
                    straight[self.at(z + 1, 1, j)] = self.at(z, 1, down)
                    self.trade(diag, self.at(z, 1, j), self.at(z + 1, 0, up))
                last = self.pairs - 1
                straight[self.at(last, 0, j)] = self.at(last, 1, j)
                straight[self.at(0, 1, j)] = self.at(0, 0, j)
            self.swap_face.append(self.full(face))
            self.straight.append(self.full(straight))
            self.diag.append(self.full(diag))
        outward, inward, cross = {}, {}, {}
        for z in zs:
            for j in js:
                after, before = (j + 1) % self.span, (j - 1) % self.span
                outward[self.at(z, 0, j)] = self.at(z, 0, after)
                outward[self.at(z, 1, j)] = self.at(z, 1, before)
                inward[self.at(z, 0, j)] = self.at(z, 0, before)
                inward[self.at(z, 1, j)] = self.at(z, 1, after)
                self.trade(cross, self.at(z, 1, j), self.at(z, 0, after))
        self.outward, self.inward, self.cross = map(self.full, (outward, inward, cross))

    def at(self, z, x, j):
        return (2 * z + x) * self.span + j

    def trade(self, moves, a, b):
        moves[a], moves[b] = b, a

    def full(self, moves):
        return [(d, moves.get(d, d ^ 1)) for d in range(self.stream * self.span)]


def place():
    s = lax.axis_index("stream")
    return s // 2, lax.rem(s, 2), lax.axis_index("span")


def is_low(rows):
    return lax.broadcasted_iota(jnp.int32, (rows, LANES), 1) < HALF


def split2(values):
    high = values.astype(bf16)
    return high, (values - high.astype(f32)).astype(bf16)


def dot(a, b, dims=((1,), (0,))):
    return lax.dot_general(a, b, (dims, ((), ())), preferred_element_type=f32)


def permuted(matrix, block):
    both = dot(matrix, jnp.concatenate(split2(block), axis=1))
    return both[:, :LANES] + both[:, LANES:]


def half_turn(block):
    return pltpu.roll(block, HALF, 1)


def pack(block, high):
    rows = block.shape[0] // 2
    return jnp.where(
        is_low(rows),
        pltpu.roll(block[:rows], HALF * high, 1),
        pltpu.roll(block[rows:], HALF * (1 - high), 1),
    )


def unpack(packed, high):
    return jnp.concatenate(
        [pltpu.roll(packed, HALF * high, 1), pltpu.roll(packed, HALF * (1 - high), 1)], axis=0
    )


def unpack2(for_low, for_high):
    low = is_low(for_low.shape[0])
    return jnp.concatenate(
        [
            jnp.where(low, for_low, half_turn(for_high)),
            jnp.where(low, half_turn(for_low), for_high),
        ],
        axis=0,
    )


def padded(plan, half):
    gap = plan.packed - half.shape[0]
    return jnp.concatenate([half, jnp.zeros((gap, LANES), f32)], axis=0) if gap else half


def spread(plan, block):
    half = plan.rows // 2
    if plan.packed == half:
        return block
    return jnp.concatenate([padded(plan, block[:half]), padded(plan, block[half:])], axis=0)


def gathered(plan, slots):
    half = plan.rows // 2
    if plan.packed == half:
        return slots
    return jnp.concatenate([slots[:half], slots[plan.packed : plan.packed + half]], axis=0)


def pairing(plan, own, arrived, x):
    return jnp.where(jnp.logical_xor(is_low(plan.rows), x == 1), own, unpack(arrived, 1 - x))


def picks(lanes):
    shape = (8 * len(lanes), NC * LANES)
    row = lax.broadcasted_iota(jnp.int32, shape, 0)
    lane = lax.broadcasted_iota(jnp.int32, shape, 1)
    hit = row < 0
    for i, at in enumerate(lanes):
        for c in range(NC):
            hit = hit | ((row == 8 * i + c) & (lane == c * LANES + at))
    return jnp.where(hit, 1.0, 0.0).astype(bf16)


def edges_of(blocks, lanes):
    blocks = jnp.concatenate([block.astype(bf16) for block in blocks], axis=1)
    return dot(picks(lanes), blocks, ((1,), (1,)))


def edges_at(edges, lanes):
    return dot(edges.astype(bf16), picks(lanes), ((0,), (0,)))


def put_edge(plan, out_ref, i, edge):
    at = NC * plan.rows // 2 + i * plan.edge_rows
    for start in range(0, plan.rows, LANES):
        width = min(LANES, plan.rows - start)
        out_ref[at : at + 8, :width] = edge[:, start : start + width]
        if width < LANES:
            out_ref[at : at + 8, width:] = jnp.zeros((8, LANES - width), f32)
        at += 8


def get_edge(plan, ref, i):
    at = NC * plan.rows // 2 + i * plan.edge_rows
    parts = []
    for start in range(0, plan.rows, LANES):
        parts.append(ref[at : at + 8, : min(LANES, plan.rows - start)])
        at += 8
    return jnp.concatenate(parts, axis=1)


def lateral(block):
    cell = lax.broadcasted_iota(jnp.int32, block.shape, 1) & (HALF - 1)
    left = jnp.where(cell == 0, 0.0, pltpu.roll(block, 1, 1))
    right = jnp.where(cell == HALF - 1, 0.0, pltpu.roll(block, LANES - 1, 1))
    return left + right - 2.0 * block


def coefficients(c):
    down = -0.5 * ADVECTION[c] + DISSIPATION[c]
    up = 0.5 * ADVECTION[c] + DISSIPATION[c]
    return down, up


def pack_kernel(block_ref, out_ref):
    _, x, _ = place()
    for c in range(NC):
        out_ref[c] = pack(block_ref[c], 1 - x)


def slot_kernel(plan, source_ref, put_ref, get_ref):
    rows, span, chips = plan.rows, plan.span, plan.chips
    z, _, j = place()
    source = source_ref[...]
    own_chip, own_core = j // 2, lax.rem(j, 2)

    def order(other, sign):
        core = jnp.where(other % 2 == own_core, 0, 1)
        turn = lax.rem(sign * (other // 2 - own_chip) + chips, chips)
        return ((core * chips + turn) * plan.part_pad).astype(f32)

    sub = lax.broadcasted_iota(jnp.int32, (rows, rows), 0)
    lane = lax.broadcasted_iota(jnp.int32, (rows, rows), 1)
    before = jnp.where(sub < lane, 1.0, 0.0).astype(bf16)
    arrival = jnp.zeros(source.shape, f32)
    base = jnp.zeros(source.shape, f32)
    for d in range(span):
        here = jnp.where((source >= d * rows) & (source < (d + 1) * rows), 1.0, 0.0)
        arrival += here * dot(here.astype(bf16), before)
        base += here * order(d, -1)
    late = jnp.where(arrival >= plan.part, 1.0, 0.0)
    within = arrival + late * (plan.packed - plan.part)
    own = lax.broadcasted_iota(jnp.int32, source.shape, 0) == j
    stator_row = jnp.sum(jnp.where(own, base + within, 0.0), axis=0, keepdims=True)
    total = jnp.zeros((rows, rows), f32)
    for d in range(span):
        match = source[d : d + 1] - j * rows == sub
        total += jnp.where(match, within[d : d + 1] + order(d, 1), 0.0)
    rotor_col = jnp.sum(total, axis=1, keepdims=True)
    same = sub == lane
    stator_col = jnp.sum(jnp.where(same, stator_row, 0.0), axis=1, keepdims=True)
    rotor_row = jnp.sum(jnp.where(same, rotor_col, 0.0), axis=0, keepdims=True)
    stator = z == plan.inlet
    col = jnp.where(stator, stator_col, rotor_col).astype(jnp.int32)
    row = jnp.where(stator, stator_row, rotor_row).astype(jnp.int32)
    put = lax.broadcasted_iota(jnp.int32, (plan.slots, rows), 0) == row
    get = lax.broadcasted_iota(jnp.int32, (rows, plan.slots), 1) == col
    put_ref[...] = jnp.where(put, 1.0, 0.0).astype(bf16)
    get_ref[...] = jnp.where(get, 1.0, 0.0).astype(bf16)


def carried_kernel(plan, adjoint_ref, inverse_ref, carried_ref):
    size = plan.block_rows
    for b in range(plan.blocks):
        rounded = jnp.concatenate(
            [adjoint_ref[c, b * size : (b + 1) * size].astype(bf16) for c in range(NC)], axis=0
        )
        product = dot(inverse_ref[b], rounded, ((0,), (0,)))
        for c in range(NC):
            carried_ref[c, b * size : (b + 1) * size] = product[c * size : (c + 1) * size]


def edge_kernel(plan, block_ref, outward_ref, inward_ref, partner_ref, own_ref):
    _, x, _ = place()
    blocks = [jnp.tanh(block_ref[c]) for c in range(NC)]
    edges = edges_of(blocks, [127 * (1 - x), 127 * x, 63 + x, 64 - x])
    for i, ref in enumerate((outward_ref, inward_ref, partner_ref, own_ref)):
        ref[...] = edges[8 * i : 8 * i + 8]


def share_kernel(plan, carried_ref, partner_ref, inward_ref, *refs):
    out_ref = refs[-1]
    _, x, _ = place()
    half = plan.rows // 2
    for c in range(NC):
        out_ref[c * half : (c + 1) * half] = pack(carried_ref[c], 1 - x)
    put_edge(plan, out_ref, 0, partner_ref[...])
    put_edge(plan, out_ref, 1, inward_ref[...])


def in_slots(plan, block, put):
    z, _, _ = place()
    low = is_low(plan.slots)
    face = jnp.logical_or(
        jnp.logical_and(low, z == plan.inlet),
        jnp.logical_and(jnp.logical_not(low), z == plan.inlet - 1),
    )
    return jnp.where(face, permuted(put, block), spread(plan, block))


def sending(plan, slots):
    turned = half_turn(slots)
    low, n = is_low(plan.packed), plan.packed
    to_before = jnp.where(low, slots[:n], turned[n:])
    to_after = jnp.where(low, turned[:n], slots[n:])
    return to_before, to_after


def put_parts(plan, ref, c, packed):
    for core in range(2):
        for turn in range(plan.chips):
            at = (core * plan.chips + turn) * plan.part_pad
            ref[core, turn, c] = packed[at : at + plan.part_pad]


def get_parts(plan, refs, c):
    parts = [refs[t][core, c] for core in range(2) for t in range(plan.chips)]
    return jnp.concatenate(parts, axis=0)


def first_kernel(plan, block_ref, arrived_ref, put_ref, flux_ref, face_ref, *z_refs):
    z, x, _ = place()
    odd = lax.rem(z, 2) == 1
    put = put_ref[...]
    half = plan.rows // 2
    for c in range(NC):
        flux = jnp.tanh(pairing(plan, block_ref[c], arrived_ref[c], x))
        flux_ref[c] = flux
        to_before, to_after = sending(plan, in_slots(plan, flux, put))
        swap = jnp.where(odd, to_before, to_after)
        other = jnp.where(odd, to_after, to_before)
        z_refs[0][c] = swap[:half]
        if len(z_refs) > 1:
            z_refs[1][c] = other[:half]
        put_parts(plan, face_ref, c, other)


def local_kernel(
    plan, block_ref, arrived_ref, flux_ref, carried_ref, share_ref, *refs
):
    outward_ref, own_ref, base_ref, pair_ref, tangent_ref = refs
    _, x, _ = place()
    half = plan.rows // 2
    low = is_low(plan.rows)
    forwarded, partner = get_edge(plan, share_ref, 1), get_edge(plan, share_ref, 0)
    edges = jnp.concatenate([outward_ref[...], forwarded, partner, own_ref[...]], axis=0)
    ghosts = edges_at(edges, [127 * x, 64 - x, 127 * (1 - x), 63 + x])
    for c in range(NC):
        own, flux = block_ref[c], flux_ref[c]
        state = pairing(plan, own, arrived_ref[c], x)
        down, up = coefficients(c)
        ghost = ghosts[:, c * LANES : (c + 1) * LANES]
        change = (
            jnp.where(low, down, up) * half_turn(flux)
            - 2.0 * DISSIPATION[c] * flux
            + SPREADING[c] * (lateral(flux) + ghost)
        )
        base_ref[c] = state + time_step * change
        share = share_ref[c * half : (c + 1) * half]
        pair_ref[c] = pairing(plan, carried_ref[c], share, x)
        flux = jnp.tanh(own)
        tangent_ref[c] = time_step * (1.0 - flux * flux)


def second_kernel(plan, base_ref, pair_ref, flux_ref, get_ref, put_ref, *refs):
    chips, count = plan.chips, len(plan.swap_z)
    face_refs, z_refs = refs[:chips], refs[chips : chips + count]
    weighted_ref, slots_ref, core_ref, partial_ref = refs[chips + count :]
    z, x, _ = place()
    odd = lax.rem(z, 2) == 1
    low = is_low(plan.rows)
    swapped = jnp.logical_xor(low, jnp.logical_not(odd))
    at_face = jnp.logical_or(z == plan.inlet, z == plan.inlet - 1)
    at_end = jnp.logical_or(z == 0, z == plan.pairs - 1)
    put, get = put_ref[...], get_ref[...]
    for c in range(NC):
        face = get_parts(plan, face_refs, c)
        near = padded(plan, z_refs[0][c])
        slots = unpack2(jnp.where(odd, near, face), jnp.where(odd, face, near))
        moved = permuted(get, slots)
        if count > 1:
            far = padded(plan, z_refs[1][c])
            slots = unpack2(jnp.where(odd, near, far), jnp.where(odd, far, near))
        slots = gathered(plan, slots)
        other = jnp.where(at_face, moved, jnp.where(at_end, 0.0, slots))
        halo = jnp.where(swapped, slots, other)
        down, up = coefficients(c)
        slope = jnp.tanh(base_ref[c] + time_step * jnp.where(low, up, down) * halo)
        weighted = (2.0 - slope * slope) * pair_ref[c]
        weighted_ref[c] = weighted
        flux = flux_ref[c]
        change = (
            jnp.where(low, up, down) * half_turn(weighted)
            - 2.0 * DISSIPATION[c] * weighted
            + SPREADING[c] * lateral(weighted)
        )
        partial = weighted + time_step * (1.0 - flux * flux) * change
        partial_ref[c] = partial
        slots = in_slots(plan, weighted, put)
        slots_ref[c] = slots
        to_before, to_after = sending(plan, slots)
        face = jnp.where(z < plan.inlet, to_after, to_before)
        for turn in range(chips):
            at = (chips + turn) * plan.part_pad
            core_ref[turn, c] = face[at : at + plan.part_pad]


def halo_kernel(plan, weighted_ref, partial_ref, slots_ref, *outs):
    out_ref, straight_ref, diag_ref, *edge_refs = outs
    _, x, _ = place()
    half = plan.rows // 2
    edges = edges_of(
        [weighted_ref[c] for c in range(NC)], [127 * (1 - x), 64 - x, 127 * x, 63 + x]
    )
    put_edge(plan, out_ref, 0, edges[:8])
    for i, ref in enumerate(edge_refs):
        ref[...] = edges[8 * i + 8 : 8 * i + 16]
    for c in range(NC):
        out_ref[c * half : (c + 1) * half] = pack(partial_ref[c], 1 - x)
        to_before, to_after = sending(plan, slots_ref[c])
        put_parts(plan, straight_ref, c, jnp.where(x == 0, to_after, to_before))
        put_parts(plan, diag_ref, c, jnp.where(x == 0, to_before, to_after))


def ghost_kernel(plan, tangent_ref, cross_ref, inward_ref, own_ref, ghost_ref):
    _, x, _ = place()
    edges = jnp.concatenate([cross_ref[...], inward_ref[...], own_ref[...]], axis=0)
    ghosts = edges_at(edges, [127 * x, 127 * (1 - x), 64 - x])
    for c in range(NC):
        ghost = ghosts[:, c * LANES : (c + 1) * LANES]
        ghost_ref[c] = tangent_ref[c] * (SPREADING[c] * ghost)


def last_kernel(plan, partial_ref, ghost_ref, tangent_ref, get_ref, share_ref, *refs):
    chips = plan.chips
    straight_refs, diag_refs, out_ref = refs[:chips], refs[chips : 2 * chips], refs[2 * chips]
    z, x, _ = place()
    half = plan.rows // 2
    first = x == 0
    at_face = z == jnp.where(first, plan.inlet, plan.inlet - 1)
    at_end = z == jnp.where(first, 0, plan.pairs - 1)
    get = get_ref[...]
    ghosts = edges_at(get_edge(plan, share_ref, 0), [63 + x])
    for c in range(NC):
        straight = get_parts(plan, straight_refs, c)
        diag = get_parts(plan, diag_refs, c)
        slots = unpack2(jnp.where(first, straight, diag), jnp.where(first, diag, straight))
        moved = permuted(get, slots)
        halo = jnp.where(at_face, moved, jnp.where(at_end, 0.0, gathered(plan, slots)))
        down, up = coefficients(c)
        ghost = ghosts[:, c * LANES : (c + 1) * LANES]
        change = jnp.where(first, down, up) * halo + SPREADING[c] * ghost
        share = share_ref[c * half : (c + 1) * half]
        partial = pairing(plan, partial_ref[c], share, x) + ghost_ref[c]
        out_ref[c] = partial + tangent_ref[c] * change


def call(kernel, outs, *args, flops=None):
    whole = pl.BlockSpec(memory_space=pltpu.VMEM)
    return pl.pallas_call(
        kernel,
        out_shape=[jax.ShapeDtypeStruct(shape, dtype) for shape, dtype in outs],
        in_specs=[whole] * len(args),
        out_specs=[whole] * len(outs),
        compiler_params=pltpu.CompilerParams(vmem_limit_bytes=32 * 2**20),
        cost_estimate=flops
        and pl.CostEstimate(flops=flops, bytes_accessed=0, transcendentals=0),
    )(*args)


def solution(mesh):
    def local(checkpoint, adjoint, line_inverse, row_source):
        rows = checkpoint.shape[1]
        plan = Plan(mesh, rows, line_inverse.shape[1])
        chips = plan.chips

        def run(kernel, outs, *args, flops=None):
            return call(lambda *refs: kernel(plan, *refs), outs, *args, flops=flops)

        def send(part, moves):
            return lax.ppermute(part, AXES, moves)

        def share(edges):
            return ((NC * rows // 2 + edges * plan.edge_rows, LANES), f32)

        full = ((NC, rows, LANES), f32)
        half = ((NC, rows // 2, LANES), f32)
        edge = ((8, rows), f32)
        parts = ((2, chips, NC, plan.part_pad, LANES), f32)
        put_shape, get_shape = ((plan.slots, rows), bf16), ((rows, plan.slots), bf16)
        checkpoint = checkpoint.reshape(full[0])
        adjoint = adjoint.reshape(full[0])
        inverse = line_inverse.reshape(line_inverse.shape[1:])
        source = row_source.reshape(plan.span, rows)
        source = jnp.pad(source, ((0, -plan.span % 8), (0, 0)), constant_values=-1)

        (mine,) = call(pack_kernel, [half], checkpoint)
        state_got = send(mine, plan.swap_x)
        outward, inward, partner, own = run(edge_kernel, [edge] * 4, checkpoint)
        outward_got = send(outward, plan.outward)
        inward_got = send(inward, plan.inward)
        (carried,) = run(carried_kernel, [full], adjoint, inverse)
        put, get = run(slot_kernel, [put_shape, get_shape], source)
        (mine,) = run(share_kernel, [share(2)], carried, partner, inward_got, outward_got)
        share_got = send(mine, plan.swap_x)
        flux, face, *near = run(
            first_kernel,
            [full, parts] + [half] * len(plan.swap_z),
            *(checkpoint, state_got, put),
        )
        crossed = send(face[1], plan.swap_core)
        near_got = [send(part, moves) for part, moves in zip(near, plan.swap_z)]
        face_got = [
            send(jnp.stack([face[0, t], crossed[t]]), plan.swap_face[t]) for t in range(chips)
        ]
        base, pair, tangent = run(
            local_kernel,
            [full] * 3,
            *(checkpoint, state_got, flux, carried, share_got, outward_got, own),
        )
        weighted, slots, core, partial = run(
            second_kernel,
            [full, ((NC, plan.slots, LANES), f32), (parts[0][1:], f32), full],
            *(base, pair, flux, get, put, *face_got, *near_got),
        )
        crossed = send(core, plan.swap_core)
        mine, straight, diag, cross, inward, own = run(
            halo_kernel, [share(1), parts, parts] + [edge] * 3, weighted, partial, slots
        )
        cross_got = send(cross, plan.cross)
        inward_got = send(inward, plan.inward)
        share_got = send(mine, plan.swap_x)
        (ghost,) = run(
            ghost_kernel, [full], tangent, cross_got, inward_got, own, flops=GHOST_FLOPS
        )
        z, x, _ = place()
        turned = jnp.logical_xor(x == 0, z == plan.inlet)
        at_face = jnp.logical_or(z == plan.inlet, z == plan.inlet - 1)

        def halo(part, moves, by_face):
            other = jnp.where(by_face, crossed, part[1])
            return [send(jnp.stack([part[0, t], other[t]]), moves[t]) for t in range(chips)]

        straight_got = halo(straight, plan.straight, jnp.logical_and(at_face, turned))
        diag_got = halo(diag, plan.diag, jnp.logical_and(at_face, jnp.logical_not(turned)))
        (out,) = run(
            last_kernel,
            [full],
            *(partial, ghost, tangent, get, share_got, *straight_got, *diag_got),
        )
        return out.reshape(NC, rows, 1, LANES)

    return jax.shard_map(
        local,
        mesh=mesh,
        in_specs=(
            P(None, None, "stream", "span"),
            P(None, None, "stream", "span"),
            P("stream", None, None, None),
            P(),
        ),
        out_specs=P(None, None, "stream", "span"),
        check_vma=False,
    )
```

```python
import jax
import jax.numpy as jnp
from jax import lax
from jax.experimental import pallas as pl
from jax.experimental.pallas import tpu as pltpu
from jax.sharding import PartitionSpec as P

time_step = 0.5
ADVECTION = (1.0, 0.6, 0.8, 1.2, 0.7)
DISSIPATION = (0.3, 0.25, 0.35, 0.3, 0.4)
SPREADING = (0.4, 0.3, 0.5, 0.35, 0.45)
NC = 5
LANES = 128
HALF = 64
AXES = ("stream", "span")
f32 = jnp.float32
bf16 = jnp.bfloat16


class Plan:
    def __init__(self, mesh, rows, blocks):
        self.stream = mesh.shape["stream"]
        self.span = mesh.shape["span"]
        self.rows = rows
        self.blocks = blocks
        self.block_rows = rows // blocks
        self.pairs = self.stream // 2
        self.inlet = self.stream // 4
        assert self.stream % 4 == 0 and self.inlet % 2 == 0 and self.span % 2 == 0
        self.chips = self.span // 2
        self.capacity = rows // self.span
        self.part = self.capacity // 2
        self.part_pad = -(-self.part // 8) * 8
        self.packed = self.span * self.part_pad
        self.slots = 2 * self.packed
        self.edge_rows = 8 * -(-rows // LANES)
        zs, js = range(self.pairs), range(self.span)
        self.swap_core = self.full({})
        self.swap_x = self.full(
            {self.at(z, x, j): self.at(z, 1 - x, j) for z in zs for j in js for x in range(2)}
        )
        self.swap_z = []
        for parity in (0, 1):
            moves = {}
            for z in zs[:-1]:
                if z % 2 == parity and z + 1 != self.inlet:
                    for x in range(2):
                        for j in js:
                            self.trade(moves, self.at(z, x, j), self.at(z + 1, x, j))
            if moves:
                self.swap_z.append(self.full(moves))
        self.swap_face, self.straight, self.diag = [], [], []
        for turn in range(self.chips):
            face, straight, diag = {}, {}, {}
            for j in js:
                for z in zs[:-1]:
                    up = down = j
                    if z + 1 == self.inlet:
                        up = (j // 2 + turn) % self.chips * 2 + j % 2
                        down = (j // 2 - turn) % self.chips * 2 + j % 2
                        for x in range(2):
                            self.trade(face, self.at(z, x, j), self.at(z + 1, x, up))
                    straight[self.at(z, 0, j)] = self.at(z + 1, 0, up)
                    straight[self.at(z + 1, 1, j)] = self.at(z, 1, down)
                    self.trade(diag, self.at(z, 1, j), self.at(z + 1, 0, up))
                last = self.pairs - 1
                straight[self.at(last, 0, j)] = self.at(last, 1, j)
                straight[self.at(0, 1, j)] = self.at(0, 0, j)
            self.swap_face.append(self.full(face))
            self.straight.append(self.full(straight))
            self.diag.append(self.full(diag))
        outward, inward, cross = {}, {}, {}
        for z in zs:
            for j in js:
                after, before = (j + 1) % self.span, (j - 1) % self.span
                outward[self.at(z, 0, j)] = self.at(z, 0, after)
                outward[self.at(z, 1, j)] = self.at(z, 1, before)
                inward[self.at(z, 0, j)] = self.at(z, 0, before)
                inward[self.at(z, 1, j)] = self.at(z, 1, after)
                self.trade(cross, self.at(z, 1, j), self.at(z, 0, after))
        self.outward, self.inward, self.cross = map(self.full, (outward, inward, cross))

    def at(self, z, x, j):
        return (2 * z + x) * self.span + j

    def trade(self, moves, a, b):
        moves[a], moves[b] = b, a

    def full(self, moves):
        return [(d, moves.get(d, d ^ 1)) for d in range(self.stream * self.span)]


def place():
    s = lax.axis_index("stream")
    return s // 2, lax.rem(s, 2), lax.axis_index("span")


def is_low(rows):
    return lax.broadcasted_iota(jnp.int32, (rows, LANES), 1) < HALF


def split2(values):
    high = values.astype(bf16)
    return high, (values - high.astype(f32)).astype(bf16)


def dot(a, b, dims=((1,), (0,))):
    return lax.dot_general(a, b, (dims, ((), ())), preferred_element_type=f32)


def permuted(matrix, block):
    both = dot(matrix, jnp.concatenate(split2(block), axis=1))
    return both[:, :LANES] + both[:, LANES:]


def half_turn(block):
    return pltpu.roll(block, HALF, 1)


def pack(block, high):
    rows = block.shape[0] // 2
    return jnp.where(
        is_low(rows),
        pltpu.roll(block[:rows], HALF * high, 1),
        pltpu.roll(block[rows:], HALF * (1 - high), 1),
    )


def unpack(packed, high):
    return jnp.concatenate(
        [pltpu.roll(packed, HALF * high, 1), pltpu.roll(packed, HALF * (1 - high), 1)], axis=0
    )


def unpack2(for_low, for_high):
    low = is_low(for_low.shape[0])
    return jnp.concatenate(
        [
            jnp.where(low, for_low, half_turn(for_high)),
            jnp.where(low, half_turn(for_low), for_high),
        ],
        axis=0,
    )


def padded(plan, half):
    gap = plan.packed - half.shape[0]
    return jnp.concatenate([half, jnp.zeros((gap, LANES), f32)], axis=0) if gap else half


def spread(plan, block):
    half = plan.rows // 2
    if plan.packed == half:
        return block
    return jnp.concatenate([padded(plan, block[:half]), padded(plan, block[half:])], axis=0)


def gathered(plan, slots):
    half = plan.rows // 2
    if plan.packed == half:
        return slots
    return jnp.concatenate([slots[:half], slots[plan.packed : plan.packed + half]], axis=0)


def pairing(plan, own, arrived, x):
    return jnp.where(jnp.logical_xor(is_low(plan.rows), x == 1), own, unpack(arrived, 1 - x))


def picks(lanes):
    shape = (8 * len(lanes), NC * LANES)
    row = lax.broadcasted_iota(jnp.int32, shape, 0)
    lane = lax.broadcasted_iota(jnp.int32, shape, 1)
    hit = row < 0
    for i, at in enumerate(lanes):
        for c in range(NC):
            hit = hit | ((row == 8 * i + c) & (lane == c * LANES + at))
    return jnp.where(hit, 1.0, 0.0).astype(bf16)


def edges_of(blocks, lanes):
    blocks = jnp.concatenate([block.astype(bf16) for block in blocks], axis=1)
    return dot(picks(lanes), blocks, ((1,), (1,)))


def edges_at(edges, lanes):
    return dot(edges.astype(bf16), picks(lanes), ((0,), (0,)))


def put_edge(plan, out_ref, i, edge):
    at = NC * plan.rows // 2 + i * plan.edge_rows
    for start in range(0, plan.rows, LANES):
        width = min(LANES, plan.rows - start)
        out_ref[at : at + 8, :width] = edge[:, start : start + width]
        if width < LANES:
            out_ref[at : at + 8, width:] = jnp.zeros((8, LANES - width), f32)
        at += 8


def get_edge(plan, ref, i):
    at = NC * plan.rows // 2 + i * plan.edge_rows
    parts = []
    for start in range(0, plan.rows, LANES):
        parts.append(ref[at : at + 8, : min(LANES, plan.rows - start)])
        at += 8
    return jnp.concatenate(parts, axis=1)


def lateral(block):
    cell = lax.broadcasted_iota(jnp.int32, block.shape, 1) & (HALF - 1)
    left = jnp.where(cell == 0, 0.0, pltpu.roll(block, 1, 1))
    right = jnp.where(cell == HALF - 1, 0.0, pltpu.roll(block, LANES - 1, 1))
    return left + right - 2.0 * block


def coefficients(c):
    down = -0.5 * ADVECTION[c] + DISSIPATION[c]
    up = 0.5 * ADVECTION[c] + DISSIPATION[c]
    return down, up


def pack_kernel(block_ref, out_ref):
    _, x, _ = place()
    for c in range(NC):
        out_ref[c] = pack(block_ref[c], 1 - x)


def slot_kernel(plan, source_ref, put_ref, get_ref):
    rows, span, chips = plan.rows, plan.span, plan.chips
    z, _, j = place()
    source = source_ref[...]
    own_chip, own_core = j // 2, lax.rem(j, 2)

    def order(other, sign):
        core = jnp.where(other % 2 == own_core, 0, 1)
        turn = lax.rem(sign * (other // 2 - own_chip) + chips, chips)
        return ((core * chips + turn) * plan.part_pad).astype(f32)

    sub = lax.broadcasted_iota(jnp.int32, (rows, rows), 0)
    lane = lax.broadcasted_iota(jnp.int32, (rows, rows), 1)
    before = jnp.where(sub < lane, 1.0, 0.0).astype(bf16)
    arrival = jnp.zeros(source.shape, f32)
    base = jnp.zeros(source.shape, f32)
    for d in range(span):
        here = jnp.where((source >= d * rows) & (source < (d + 1) * rows), 1.0, 0.0)
        arrival += here * dot(here.astype(bf16), before)
        base += here * order(d, -1)
    late = jnp.where(arrival >= plan.part, 1.0, 0.0)
    within = arrival + late * (plan.packed - plan.part)
    own = lax.broadcasted_iota(jnp.int32, source.shape, 0) == j
    stator_row = jnp.sum(jnp.where(own, base + within, 0.0), axis=0, keepdims=True)
    total = jnp.zeros((rows, rows), f32)
    for d in range(span):
        match = source[d : d + 1] - j * rows == sub
        total += jnp.where(match, within[d : d + 1] + order(d, 1), 0.0)
    rotor_col = jnp.sum(total, axis=1, keepdims=True)
    same = sub == lane
    stator_col = jnp.sum(jnp.where(same, stator_row, 0.0), axis=1, keepdims=True)
    rotor_row = jnp.sum(jnp.where(same, rotor_col, 0.0), axis=0, keepdims=True)
    stator = z == plan.inlet
    col = jnp.where(stator, stator_col, rotor_col).astype(jnp.int32)
    row = jnp.where(stator, stator_row, rotor_row).astype(jnp.int32)
    put = lax.broadcasted_iota(jnp.int32, (plan.slots, rows), 0) == row
    get = lax.broadcasted_iota(jnp.int32, (rows, plan.slots), 1) == col
    put_ref[...] = jnp.where(put, 1.0, 0.0).astype(bf16)
    get_ref[...] = jnp.where(get, 1.0, 0.0).astype(bf16)


def carried_kernel(plan, adjoint_ref, inverse_ref, carried_ref):
    size = plan.block_rows
    for b in range(plan.blocks):
        rounded = jnp.concatenate(
            [adjoint_ref[c, b * size : (b + 1) * size].astype(bf16) for c in range(NC)], axis=0
        )
        product = dot(inverse_ref[b], rounded, ((0,), (0,)))
        for c in range(NC):
            carried_ref[c, b * size : (b + 1) * size] = product[c * size : (c + 1) * size]


def edge_kernel(plan, block_ref, outward_ref, inward_ref, partner_ref, own_ref):
    _, x, _ = place()
    blocks = [jnp.tanh(block_ref[c]) for c in range(NC)]
    edges = edges_of(blocks, [127 * (1 - x), 127 * x, 63 + x, 64 - x])
    for i, ref in enumerate((outward_ref, inward_ref, partner_ref, own_ref)):
        ref[...] = edges[8 * i : 8 * i + 8]


def share_kernel(plan, carried_ref, partner_ref, inward_ref, *refs):
    out_ref = refs[-1]
    _, x, _ = place()
    half = plan.rows // 2
    for c in range(NC):
        out_ref[c * half : (c + 1) * half] = pack(carried_ref[c], 1 - x)
    put_edge(plan, out_ref, 0, partner_ref[...])
    put_edge(plan, out_ref, 1, inward_ref[...])


def in_slots(plan, block, put):
    z, _, _ = place()
    low = is_low(plan.slots)
    face = jnp.logical_or(
        jnp.logical_and(low, z == plan.inlet),
        jnp.logical_and(jnp.logical_not(low), z == plan.inlet - 1),
    )
    return jnp.where(face, permuted(put, block), spread(plan, block))


def sending(plan, slots):
    turned = half_turn(slots)
    low, n = is_low(plan.packed), plan.packed
    to_before = jnp.where(low, slots[:n], turned[n:])
    to_after = jnp.where(low, turned[:n], slots[n:])
    return to_before, to_after


def put_parts(plan, ref, c, packed):
    for core in range(2):
        for turn in range(plan.chips):
            at = (core * plan.chips + turn) * plan.part_pad
            ref[core, turn, c] = packed[at : at + plan.part_pad]


def get_parts(plan, refs, c):
    parts = [refs[t][core, c] for core in range(2) for t in range(plan.chips)]
    return jnp.concatenate(parts, axis=0)


def first_kernel(plan, block_ref, arrived_ref, put_ref, flux_ref, face_ref, *z_refs):
    z, x, _ = place()
    odd = lax.rem(z, 2) == 1
    put = put_ref[...]
    half = plan.rows // 2
    for c in range(NC):
        flux = jnp.tanh(pairing(plan, block_ref[c], arrived_ref[c], x))
        flux_ref[c] = flux
        to_before, to_after = sending(plan, in_slots(plan, flux, put))
        swap = jnp.where(odd, to_before, to_after)
        other = jnp.where(odd, to_after, to_before)
        z_refs[0][c] = swap[:half]
        if len(z_refs) > 1:
            z_refs[1][c] = other[:half]
        put_parts(plan, face_ref, c, other)


def local_kernel(
    plan, block_ref, arrived_ref, flux_ref, carried_ref, share_ref, *refs
):
    outward_ref, own_ref, base_ref, pair_ref, tangent_ref = refs
    _, x, _ = place()
    half = plan.rows // 2
    low = is_low(plan.rows)
    forwarded, partner = get_edge(plan, share_ref, 1), get_edge(plan, share_ref, 0)
    edges = jnp.concatenate([outward_ref[...], forwarded, partner, own_ref[...]], axis=0)
    ghosts = edges_at(edges, [127 * x, 64 - x, 127 * (1 - x), 63 + x])
    for c in range(NC):
        own, flux = block_ref[c], flux_ref[c]
        state = pairing(plan, own, arrived_ref[c], x)
        down, up = coefficients(c)
        ghost = ghosts[:, c * LANES : (c + 1) * LANES]
        change = (
            jnp.where(low, down, up) * half_turn(flux)
            - 2.0 * DISSIPATION[c] * flux
            + SPREADING[c] * (lateral(flux) + ghost)
        )
        base_ref[c] = state + time_step * change
        share = share_ref[c * half : (c + 1) * half]
        pair_ref[c] = pairing(plan, carried_ref[c], share, x)
        flux = jnp.tanh(own)
        tangent_ref[c] = time_step * (1.0 - flux * flux)


def second_kernel(plan, base_ref, pair_ref, flux_ref, get_ref, put_ref, *refs):
    chips, count = plan.chips, len(plan.swap_z)
    face_refs, z_refs = refs[:chips][::-1], refs[chips : chips + count]
    weighted_ref, slots_ref, core_ref, partial_ref = refs[chips + count :]
    z, x, _ = place()
    odd = lax.rem(z, 2) == 1
    low = is_low(plan.rows)
    swapped = jnp.logical_xor(low, jnp.logical_not(odd))
    at_face = jnp.logical_or(z == plan.inlet, z == plan.inlet - 1)
    at_end = jnp.logical_or(z == 0, z == plan.pairs - 1)
    put, get = put_ref[...], get_ref[...]
    for c in range(NC):
        face = get_parts(plan, face_refs, c)
        near = padded(plan, z_refs[0][c])
        slots = unpack2(jnp.where(odd, near, face), jnp.where(odd, face, near))
        moved = permuted(get, slots)
        if count > 1:
            far = padded(plan, z_refs[1][c])
            slots = unpack2(jnp.where(odd, near, far), jnp.where(odd, far, near))
        slots = gathered(plan, slots)
        other = jnp.where(at_face, moved, jnp.where(at_end, 0.0, slots))
        halo = jnp.where(swapped, slots, other)
        down, up = coefficients(c)
        slope = jnp.tanh(base_ref[c] + time_step * jnp.where(low, up, down) * halo)
        weighted = (2.0 - slope * slope) * pair_ref[c]
        weighted_ref[c] = weighted
        flux = flux_ref[c]
        change = (
            jnp.where(low, up, down) * half_turn(weighted)
            - 2.0 * DISSIPATION[c] * weighted
            + SPREADING[c] * lateral(weighted)
        )
        partial = weighted + time_step * (1.0 - flux * flux) * change
        partial_ref[c] = partial
        slots = in_slots(plan, weighted, put)
        slots_ref[c] = slots
        to_before, to_after = sending(plan, slots)
        face = jnp.where(z < plan.inlet, to_after, to_before)
        for turn in range(chips):
            at = (chips + turn) * plan.part_pad
            core_ref[turn, c] = face[at : at + plan.part_pad]


def halo_kernel(plan, weighted_ref, partial_ref, slots_ref, *outs):
    out_ref, straight_ref, diag_ref, *edge_refs = outs
    _, x, _ = place()
    half = plan.rows // 2
    edges = edges_of(
        [weighted_ref[c] for c in range(NC)], [127 * (1 - x), 64 - x, 127 * x, 63 + x]
    )
    put_edge(plan, out_ref, 0, edges[:8])
    for i, ref in enumerate(edge_refs):
        ref[...] = edges[8 * i + 8 : 8 * i + 16]
    for c in range(NC):
        out_ref[c * half : (c + 1) * half] = pack(partial_ref[c], 1 - x)
        to_before, to_after = sending(plan, slots_ref[c])
        put_parts(plan, straight_ref, c, jnp.where(x == 0, to_after, to_before))
        put_parts(plan, diag_ref, c, jnp.where(x == 0, to_before, to_after))


def ghost_kernel(plan, rest_ref, tangent_ref, cross_ref, inward_ref, own_ref, ghost_ref):
    _, x, _ = place()
    edges = jnp.concatenate([cross_ref[...], inward_ref[...], own_ref[...]], axis=0)
    ghosts = edges_at(edges, [127 * x, 127 * (1 - x), 64 - x])
    for c in range(NC):
        ghost = ghosts[:, c * LANES : (c + 1) * LANES]
        ghost_ref[c] = rest_ref[c] + tangent_ref[c] * (SPREADING[c] * ghost)


def rest_kernel(plan, tangent_ref, get_ref, *refs):
    chips = plan.chips
    diag_refs, straight_refs, rest_ref = refs[:chips], refs[chips : 2 * chips][::-1], refs[2 * chips]
    z, x, _ = place()
    first = x == 0
    at_face = z == jnp.where(first, plan.inlet, plan.inlet - 1)
    at_end = z == jnp.where(first, 0, plan.pairs - 1)
    get = get_ref[...]
    for c in range(NC):
        straight = get_parts(plan, straight_refs, c)
        diag = get_parts(plan, diag_refs, c)
        slots = unpack2(jnp.where(first, straight, diag), jnp.where(first, diag, straight))
        moved = permuted(get, slots)
        halo = jnp.where(at_face, moved, jnp.where(at_end, 0.0, gathered(plan, slots)))
        down, up = coefficients(c)
        rest_ref[c] = tangent_ref[c] * (jnp.where(first, down, up) * halo)


def last_kernel(plan, partial_ref, rest_ref, tangent_ref, share_ref, out_ref):
    _, x, _ = place()
    half = plan.rows // 2
    ghosts = edges_at(get_edge(plan, share_ref, 0), [63 + x])
    for c in range(NC):
        ghost = ghosts[:, c * LANES : (c + 1) * LANES]
        share = share_ref[c * half : (c + 1) * half]
        rest = rest_ref[c] + tangent_ref[c] * (SPREADING[c] * ghost)
        out_ref[c] = pairing(plan, partial_ref[c], share, x) + rest


def call(kernel, outs, *args, flops=None):
    whole = pl.BlockSpec(memory_space=pltpu.VMEM)
    return pl.pallas_call(
        kernel,
        out_shape=[jax.ShapeDtypeStruct(shape, dtype) for shape, dtype in outs],
        in_specs=[whole] * len(args),
        out_specs=[whole] * len(outs),
        compiler_params=pltpu.CompilerParams(vmem_limit_bytes=32 * 2**20),
        cost_estimate=flops
        and pl.CostEstimate(flops=flops, bytes_accessed=0, transcendentals=0),
    )(*args)


def solution(mesh):
    def local(checkpoint, adjoint, line_inverse, row_source):
        rows = checkpoint.shape[1]
        plan = Plan(mesh, rows, line_inverse.shape[1])
        chips = plan.chips

        def run(kernel, outs, *args, flops=None):
            return call(lambda *refs: kernel(plan, *refs), outs, *args, flops=flops)

        def send(part, moves):
            return lax.ppermute(part, AXES, moves)

        def share(edges):
            return ((NC * rows // 2 + edges * plan.edge_rows, LANES), f32)

        full = ((NC, rows, LANES), f32)
        half = ((NC, rows // 2, LANES), f32)
        edge = ((8, rows), f32)
        parts = ((2, chips, NC, plan.part_pad, LANES), f32)
        put_shape, get_shape = ((plan.slots, rows), bf16), ((rows, plan.slots), bf16)
        checkpoint = checkpoint.reshape(full[0])
        adjoint = adjoint.reshape(full[0])
        inverse = line_inverse.reshape(line_inverse.shape[1:])
        source = row_source.reshape(plan.span, rows)
        source = jnp.pad(source, ((0, -plan.span % 8), (0, 0)), constant_values=-1)

        (mine,) = call(pack_kernel, [half], checkpoint)
        state_got = send(mine, plan.swap_x)
        outward, inward, partner, own = run(edge_kernel, [edge] * 4, checkpoint)
        outward_got = send(outward, plan.outward)
        inward_got = send(inward, plan.inward)
        (carried,) = run(carried_kernel, [full], adjoint, inverse)
        put, get = run(slot_kernel, [put_shape, get_shape], source)
        (mine,) = run(share_kernel, [share(2)], carried, partner, inward_got, outward_got)
        share_got = send(mine, plan.swap_x)
        flux, face, *near = run(
            first_kernel,
            [full, parts] + [half] * len(plan.swap_z),
            *(checkpoint, state_got, put),
        )
        crossed = send(face[1], plan.swap_core)
        near_got = [send(part, moves) for part, moves in zip(near, plan.swap_z)]
        face_got = [
            send(jnp.stack([face[0, t], crossed[t]]), plan.swap_face[t]) for t in range(chips)
        ]
        base, pair, tangent = run(
            local_kernel,
            [full] * 3,
            *(checkpoint, state_got, flux, carried, share_got, outward_got, own),
        )
        weighted, slots, core, partial = run(
            second_kernel,
            [full, ((NC, plan.slots, LANES), f32), (parts[0][1:], f32), full],
            *(base, pair, flux, get, put, *face_got[::-1], *near_got),
        )
        crossed = send(core, plan.swap_core)
        mine, straight, diag, cross, inward, own = run(
            halo_kernel, [share(1), parts, parts] + [edge] * 3, weighted, partial, slots
        )
        share_got = send(mine, plan.swap_x)
        z, x, _ = place()
        turned = jnp.logical_xor(x == 0, z == plan.inlet)
        at_face = jnp.logical_or(z == plan.inlet, z == plan.inlet - 1)

        def halo(part, moves, by_face):
            other = jnp.where(by_face, crossed, part[1])
            return [send(jnp.stack([part[0, t], other[t]]), moves[t]) for t in range(chips)]

        straight_got = halo(straight, plan.straight, jnp.logical_and(at_face, turned))
        diag_got = halo(diag, plan.diag, jnp.logical_and(at_face, jnp.logical_not(turned)))
        (cross, inward), _ = lax.optimization_barrier(((cross, inward), diag_got[0]))
        cross_got = send(cross, plan.cross)
        inward_got = send(inward, plan.inward)
        (rest,) = run(rest_kernel, [full], tangent, get, *diag_got, *straight_got[::-1])
        (ghost,) = run(ghost_kernel, [full], rest, tangent, cross_got, inward_got, own)
        (out,) = run(last_kernel, [full], partial, ghost, tangent, share_got)
        return out.reshape(NC, rows, 1, LANES)

    return jax.shard_map(
        local,
        mesh=mesh,
        in_specs=(
            P(None, None, "stream", "span"),
            P(None, None, "stream", "span"),
            P("stream", None, None, None),
            P(),
        ),
        out_specs=P(None, None, "stream", "span"),
        check_vma=False,
    )
```

```python
import jax
import jax.numpy as jnp
from jax import lax
from jax.experimental import pallas as pl
from jax.experimental.pallas import tpu as pltpu
from jax.sharding import PartitionSpec as P

time_step = 0.5
ADVECTION = (1.0, 0.6, 0.8, 1.2, 0.7)
DISSIPATION = (0.3, 0.25, 0.35, 0.3, 0.4)
SPREADING = (0.4, 0.3, 0.5, 0.35, 0.45)
NC = 5
LANES = 128
HALF = 64
AXES = ("stream", "span")
f32 = jnp.float32
bf16 = jnp.bfloat16


class Plan:
    def __init__(self, mesh, rows, blocks):
        self.stream = mesh.shape["stream"]
        self.span = mesh.shape["span"]
        self.rows = rows
        self.blocks = blocks
        self.block_rows = rows // blocks
        self.pairs = self.stream // 2
        self.inlet = self.stream // 4
        assert self.stream % 4 == 0 and self.inlet % 2 == 0 and self.span % 2 == 0
        self.chips = self.span // 2
        self.capacity = rows // self.span
        self.part = self.capacity // 2
        self.part_pad = -(-self.part // 8) * 8
        self.packed = self.span * self.part_pad
        self.slots = 2 * self.packed
        self.edge_rows = 8 * -(-rows // LANES)
        zs, js = range(self.pairs), range(self.span)
        self.swap_core = self.full({})
        self.swap_x = self.full(
            {self.at(z, x, j): self.at(z, 1 - x, j) for z in zs for j in js for x in range(2)}
        )
        self.swap_z = []
        for parity in (0, 1):
            moves = {}
            for z in zs[:-1]:
                if z % 2 == parity and z + 1 != self.inlet:
                    for x in range(2):
                        for j in js:
                            self.trade(moves, self.at(z, x, j), self.at(z + 1, x, j))
            if moves:
                self.swap_z.append(self.full(moves))
        self.swap_face, self.straight, self.diag = [], [], []
        for turn in range(self.chips):
            face, straight, diag = {}, {}, {}
            for j in js:
                for z in zs[:-1]:
                    up = down = j
                    if z + 1 == self.inlet:
                        up = (j // 2 + turn) % self.chips * 2 + j % 2
                        down = (j // 2 - turn) % self.chips * 2 + j % 2
                        for x in range(2):
                            self.trade(face, self.at(z, x, j), self.at(z + 1, x, up))
                    straight[self.at(z, 0, j)] = self.at(z + 1, 0, up)
                    straight[self.at(z + 1, 1, j)] = self.at(z, 1, down)
                    self.trade(diag, self.at(z, 1, j), self.at(z + 1, 0, up))
                last = self.pairs - 1
                straight[self.at(last, 0, j)] = self.at(last, 1, j)
                straight[self.at(0, 1, j)] = self.at(0, 0, j)
            self.swap_face.append(self.full(face))
            self.straight.append(self.full(straight))
            self.diag.append(self.full(diag))
        outward, inward, cross = {}, {}, {}
        for z in zs:
            for j in js:
                after, before = (j + 1) % self.span, (j - 1) % self.span
                outward[self.at(z, 0, j)] = self.at(z, 0, after)
                outward[self.at(z, 1, j)] = self.at(z, 1, before)
                inward[self.at(z, 0, j)] = self.at(z, 0, before)
                inward[self.at(z, 1, j)] = self.at(z, 1, after)
                self.trade(cross, self.at(z, 1, j), self.at(z, 0, after))
        self.outward, self.inward, self.cross = map(self.full, (outward, inward, cross))

    def at(self, z, x, j):
        return (2 * z + x) * self.span + j

    def trade(self, moves, a, b):
        moves[a], moves[b] = b, a

    def full(self, moves):
        return [(d, moves.get(d, d ^ 1)) for d in range(self.stream * self.span)]


def place():
    s = lax.axis_index("stream")
    return s // 2, lax.rem(s, 2), lax.axis_index("span")


def is_low(rows):
    return lax.broadcasted_iota(jnp.int32, (rows, LANES), 1) < HALF


def split2(values):
    high = values.astype(bf16)
    return high, (values - high.astype(f32)).astype(bf16)


def dot(a, b, dims=((1,), (0,))):
    return lax.dot_general(a, b, (dims, ((), ())), preferred_element_type=f32)


def permuted(matrix, block):
    both = dot(matrix, jnp.concatenate(split2(block), axis=1))
    return both[:, :LANES] + both[:, LANES:]


def half_turn(block):
    return pltpu.roll(block, HALF, 1)


def pack(block, high):
    rows = block.shape[0] // 2
    return jnp.where(
        is_low(rows),
        pltpu.roll(block[:rows], HALF * high, 1),
        pltpu.roll(block[rows:], HALF * (1 - high), 1),
    )


def unpack(packed, high):
    return jnp.concatenate(
        [pltpu.roll(packed, HALF * high, 1), pltpu.roll(packed, HALF * (1 - high), 1)], axis=0
    )


def unpack2(for_low, for_high):
    low = is_low(for_low.shape[0])
    return jnp.concatenate(
        [
            jnp.where(low, for_low, half_turn(for_high)),
            jnp.where(low, half_turn(for_low), for_high),
        ],
        axis=0,
    )


def padded(plan, half):
    gap = plan.packed - half.shape[0]
    return jnp.concatenate([half, jnp.zeros((gap, LANES), f32)], axis=0) if gap else half


def spread(plan, block):
    half = plan.rows // 2
    if plan.packed == half:
        return block
    return jnp.concatenate([padded(plan, block[:half]), padded(plan, block[half:])], axis=0)


def gathered(plan, slots):
    half = plan.rows // 2
    if plan.packed == half:
        return slots
    return jnp.concatenate([slots[:half], slots[plan.packed : plan.packed + half]], axis=0)


def pairing(plan, own, arrived, x):
    return jnp.where(jnp.logical_xor(is_low(plan.rows), x == 1), own, unpack(arrived, 1 - x))


def picks(lanes):
    shape = (8 * len(lanes), NC * LANES)
    row = lax.broadcasted_iota(jnp.int32, shape, 0)
    lane = lax.broadcasted_iota(jnp.int32, shape, 1)
    hit = row < 0
    for i, at in enumerate(lanes):
        for c in range(NC):
            hit = hit | ((row == 8 * i + c) & (lane == c * LANES + at))
    return jnp.where(hit, 1.0, 0.0).astype(bf16)


def edges_of(blocks, lanes):
    blocks = jnp.concatenate([block.astype(bf16) for block in blocks], axis=1)
    return dot(picks(lanes), blocks, ((1,), (1,)))


def edges_at(edges, lanes):
    return dot(edges.astype(bf16), picks(lanes), ((0,), (0,)))


def put_edge(plan, out_ref, i, edge):
    at = NC * plan.rows // 2 + i * plan.edge_rows
    for start in range(0, plan.rows, LANES):
        width = min(LANES, plan.rows - start)
        out_ref[at : at + 8, :width] = edge[:, start : start + width]
        if width < LANES:
            out_ref[at : at + 8, width:] = jnp.zeros((8, LANES - width), f32)
        at += 8


def get_edge(plan, ref, i):
    at = NC * plan.rows // 2 + i * plan.edge_rows
    parts = []
    for start in range(0, plan.rows, LANES):
        parts.append(ref[at : at + 8, : min(LANES, plan.rows - start)])
        at += 8
    return jnp.concatenate(parts, axis=1)


def lane_row(values):
    lane = lax.broadcasted_iota(jnp.int32, (1, LANES), 1)
    row = jnp.zeros((1, LANES), f32)
    for hit, value in values(lane):
        row = jnp.where(hit, value, row)
    return row


def lateral(block):
    inner_left = lane_row(lambda lane: [((lane & (HALF - 1)) != 0, 1.0)])
    inner_right = lane_row(lambda lane: [((lane & (HALF - 1)) != HALF - 1, 1.0)])
    left = pltpu.roll(block, 1, 1) * inner_left
    right = pltpu.roll(block, LANES - 1, 1) * inner_right
    return left + right - 2.0 * block


def halves(low, high):
    return lane_row(lambda lane: [(lane < HALF, low), (lane >= HALF, high)])


def coefficients(c):
    down = -0.5 * ADVECTION[c] + DISSIPATION[c]
    up = 0.5 * ADVECTION[c] + DISSIPATION[c]
    return down, up


def pack_kernel(block_ref, out_ref):
    _, x, _ = place()
    for c in range(NC):
        out_ref[c] = pack(block_ref[c], 1 - x)


def slot_kernel(plan, source_ref, put_ref, get_ref):
    rows, span, chips = plan.rows, plan.span, plan.chips
    z, _, j = place()
    source = source_ref[...]
    own_chip, own_core = j // 2, lax.rem(j, 2)

    def order(other, sign):
        core = jnp.where(other % 2 == own_core, 0, 1)
        turn = lax.rem(sign * (other // 2 - own_chip) + chips, chips)
        return ((core * chips + turn) * plan.part_pad).astype(f32)

    sub = lax.broadcasted_iota(jnp.int32, (rows, rows), 0)
    lane = lax.broadcasted_iota(jnp.int32, (rows, rows), 1)
    before = jnp.where(sub < lane, 1.0, 0.0).astype(bf16)
    arrival = jnp.zeros(source.shape, f32)
    base = jnp.zeros(source.shape, f32)
    for d in range(span):
        here = jnp.where((source >= d * rows) & (source < (d + 1) * rows), 1.0, 0.0)
        arrival += here * dot(here.astype(bf16), before)
        base += here * order(d, -1)
    late = jnp.where(arrival >= plan.part, 1.0, 0.0)
    within = arrival + late * (plan.packed - plan.part)
    own = lax.broadcasted_iota(jnp.int32, source.shape, 0) == j
    stator_row = jnp.sum(jnp.where(own, base + within, 0.0), axis=0, keepdims=True)
    total = jnp.zeros((rows, rows), f32)
    for d in range(span):
        match = source[d : d + 1] - j * rows == sub
        total += jnp.where(match, within[d : d + 1] + order(d, 1), 0.0)
    rotor_col = jnp.sum(total, axis=1, keepdims=True)
    same = sub == lane
    stator_col = jnp.sum(jnp.where(same, stator_row, 0.0), axis=1, keepdims=True)
    rotor_row = jnp.sum(jnp.where(same, rotor_col, 0.0), axis=0, keepdims=True)
    stator = z == plan.inlet
    col = jnp.where(stator, stator_col, rotor_col).astype(jnp.int32)
    row = jnp.where(stator, stator_row, rotor_row).astype(jnp.int32)
    put = lax.broadcasted_iota(jnp.int32, (plan.slots, rows), 0) == row
    get = lax.broadcasted_iota(jnp.int32, (rows, plan.slots), 1) == col
    put_ref[...] = jnp.where(put, 1.0, 0.0).astype(bf16)
    get = jnp.logical_and(get, jnp.logical_or(stator, z == plan.inlet - 1))
    get_ref[...] = jnp.where(get, 1.0, 0.0).astype(bf16)


def carried_kernel(plan, adjoint_ref, inverse_ref, carried_ref):
    size = plan.block_rows
    for b in range(plan.blocks):
        rounded = jnp.concatenate(
            [adjoint_ref[c, b * size : (b + 1) * size].astype(bf16) for c in range(NC)], axis=0
        )
        product = dot(inverse_ref[b], rounded, ((0,), (0,)))
        for c in range(NC):
            carried_ref[c, b * size : (b + 1) * size] = product[c * size : (c + 1) * size]


def edge_kernel(plan, block_ref, outward_ref, inward_ref, partner_ref, own_ref):
    _, x, _ = place()
    blocks = [jnp.tanh(block_ref[c]) for c in range(NC)]
    edges = edges_of(blocks, [127 * (1 - x), 127 * x, 63 + x, 64 - x])
    for i, ref in enumerate((outward_ref, inward_ref, partner_ref, own_ref)):
        ref[...] = edges[8 * i : 8 * i + 8]


def share_kernel(plan, carried_ref, partner_ref, inward_ref, *refs):
    out_ref = refs[-1]
    _, x, _ = place()
    half = plan.rows // 2
    for c in range(NC):
        out_ref[c * half : (c + 1) * half] = pack(carried_ref[c], 1 - x)
    put_edge(plan, out_ref, 0, partner_ref[...])
    put_edge(plan, out_ref, 1, inward_ref[...])


def in_slots(plan, block, put):
    z, _, _ = place()
    low = is_low(plan.slots)
    face = jnp.logical_or(
        jnp.logical_and(low, z == plan.inlet),
        jnp.logical_and(jnp.logical_not(low), z == plan.inlet - 1),
    )
    return jnp.where(face, permuted(put, block), spread(plan, block))


def sending(plan, slots):
    turned = half_turn(slots)
    low, n = is_low(plan.packed), plan.packed
    to_before = jnp.where(low, slots[:n], turned[n:])
    to_after = jnp.where(low, turned[:n], slots[n:])
    return to_before, to_after


def put_parts(plan, ref, c, packed):
    for core in range(2):
        for turn in range(plan.chips):
            at = (core * plan.chips + turn) * plan.part_pad
            ref[core, turn, c] = packed[at : at + plan.part_pad]


def get_parts(plan, refs, c):
    parts = [refs[t][core, c] for core in range(2) for t in range(plan.chips)]
    return jnp.concatenate(parts, axis=0)


def first_kernel(plan, block_ref, arrived_ref, put_ref, flux_ref, face_ref, *z_refs):
    z, x, _ = place()
    odd = lax.rem(z, 2) == 1
    put = put_ref[...]
    half = plan.rows // 2
    for c in range(NC):
        flux = jnp.tanh(pairing(plan, block_ref[c], arrived_ref[c], x))
        flux_ref[c] = flux
        to_before, to_after = sending(plan, in_slots(plan, flux, put))
        swap = jnp.where(odd, to_before, to_after)
        other = jnp.where(odd, to_after, to_before)
        z_refs[0][c] = swap[:half]
        if len(z_refs) > 1:
            z_refs[1][c] = other[:half]
        put_parts(plan, face_ref, c, other)


def local_kernel(
    plan, block_ref, arrived_ref, flux_ref, carried_ref, share_ref, *refs
):
    outward_ref, own_ref, base_ref, pair_ref, tangent_ref, pair_tangent_ref = refs
    _, x, _ = place()
    half = plan.rows // 2
    low = is_low(plan.rows)
    forwarded, partner = get_edge(plan, share_ref, 1), get_edge(plan, share_ref, 0)
    edges = jnp.concatenate([outward_ref[...], forwarded, partner, own_ref[...]], axis=0)
    ghosts = edges_at(edges, [127 * x, 64 - x, 127 * (1 - x), 63 + x])
    for c in range(NC):
        own, flux = block_ref[c], flux_ref[c]
        state = pairing(plan, own, arrived_ref[c], x)
        down, up = coefficients(c)
        ghost = ghosts[:, c * LANES : (c + 1) * LANES]
        change = (
            halves(down, up) * half_turn(flux)
            - 2.0 * DISSIPATION[c] * flux
            + SPREADING[c] * (lateral(flux) + ghost)
        )
        base_ref[c] = state + time_step * change
        pair_tangent_ref[c] = time_step * (1.0 - flux * flux)
        share = share_ref[c * half : (c + 1) * half]
        pair_ref[c] = pairing(plan, carried_ref[c], share, x)
        flux = jnp.tanh(own)
        tangent_ref[c] = time_step * (1.0 - flux * flux)


def second_kernel(plan, base_ref, pair_ref, tangent_ref, get_ref, put_ref, *refs):
    chips, count = plan.chips, len(plan.swap_z)
    face_refs, z_refs = refs[:chips][::-1], refs[chips : chips + count]
    core_ref, partial_ref, out_ref, straight_ref, diag_ref, *edge_refs = refs[chips + count :]
    z, x, _ = place()
    odd = lax.rem(z, 2) == 1
    low = is_low(plan.rows)
    swapped = jnp.logical_xor(low, jnp.logical_not(odd))
    at_face = jnp.logical_or(z == plan.inlet, z == plan.inlet - 1)
    at_end = jnp.logical_or(z == 0, z == plan.pairs - 1)
    put, get = put_ref[...], get_ref[...]
    half = plan.rows // 2
    blocks = []
    for c in range(NC):
        face = get_parts(plan, face_refs, c)
        near = padded(plan, z_refs[0][c])
        slots = unpack2(jnp.where(odd, near, face), jnp.where(odd, face, near))
        moved = permuted(get, slots)
        if count > 1:
            far = padded(plan, z_refs[1][c])
            slots = unpack2(jnp.where(odd, near, far), jnp.where(odd, far, near))
            far = jnp.where(jnp.logical_or(at_face, at_end), moved, gathered(plan, slots))
        else:
            far = moved
        halo = jnp.where(swapped, gathered(plan, slots), far)
        down, up = coefficients(c)
        slope = jnp.tanh(base_ref[c] + halves(time_step * up, time_step * down) * halo)
        weighted = (2.0 - slope * slope) * pair_ref[c]
        change = (
            halves(up, down) * half_turn(weighted)
            - 2.0 * DISSIPATION[c] * weighted
            + SPREADING[c] * lateral(weighted)
        )
        partial = weighted + tangent_ref[c] * change
        partial_ref[c] = partial
        out_ref[c * half : (c + 1) * half] = pack(partial, 1 - x)
        to_before, to_after = sending(plan, in_slots(plan, weighted, put))
        put_parts(plan, straight_ref, c, jnp.where(x == 0, to_after, to_before))
        put_parts(plan, diag_ref, c, jnp.where(x == 0, to_before, to_after))
        face = jnp.where(z < plan.inlet, to_after, to_before)
        for turn in range(chips):
            at = (chips + turn) * plan.part_pad
            core_ref[turn, c] = face[at : at + plan.part_pad]
        blocks.append(weighted)
    edges = edges_of(blocks, [127 * (1 - x), 64 - x, 127 * x, 63 + x])
    put_edge(plan, out_ref, 0, edges[:8])
    for i, ref in enumerate(edge_refs):
        ref[...] = edges[8 * i + 8 : 8 * i + 16]


def rest_kernel(plan, tangent_ref, get_ref, *refs):
    chips = plan.chips
    diag_refs, straight_refs, rest_ref = refs[:chips], refs[chips : 2 * chips][::-1], refs[2 * chips]
    z, x, _ = place()
    first = x == 0
    at_face = z == jnp.where(first, plan.inlet, plan.inlet - 1)
    at_end = z == jnp.where(first, 0, plan.pairs - 1)
    get = get_ref[...]
    for c in range(NC):
        straight = get_parts(plan, straight_refs, c)
        diag = get_parts(plan, diag_refs, c)
        slots = unpack2(jnp.where(first, straight, diag), jnp.where(first, diag, straight))
        moved = permuted(get, slots)
        halo = jnp.where(at_face, moved, jnp.where(at_end, 0.0, gathered(plan, slots)))
        down, up = coefficients(c)
        rest_ref[c] = tangent_ref[c] * (jnp.where(first, down, up) * halo)


def last_kernel(plan, partial_ref, rest_ref, tangent_ref, share_ref, *refs):
    cross_ref, inward_ref, own_ref, out_ref = refs
    _, x, _ = place()
    half = plan.rows // 2
    edges = [get_edge(plan, share_ref, 0), cross_ref[...], inward_ref[...], own_ref[...]]
    ghosts = edges_at(
        jnp.concatenate(edges, axis=0), [63 + x, 127 * x, 127 * (1 - x), 64 - x]
    )
    for c in range(NC):
        ghost = ghosts[:, c * LANES : (c + 1) * LANES]
        share = share_ref[c * half : (c + 1) * half]
        rest = rest_ref[c] + tangent_ref[c] * (SPREADING[c] * ghost)
        out_ref[c] = pairing(plan, partial_ref[c], share, x) + rest


def call(kernel, outs, *args, flops=None):
    whole = pl.BlockSpec(memory_space=pltpu.VMEM)
    return pl.pallas_call(
        kernel,
        out_shape=[jax.ShapeDtypeStruct(shape, dtype) for shape, dtype in outs],
        in_specs=[whole] * len(args),
        out_specs=[whole] * len(outs),
        compiler_params=pltpu.CompilerParams(vmem_limit_bytes=32 * 2**20),
        cost_estimate=flops
        and pl.CostEstimate(flops=flops, bytes_accessed=0, transcendentals=0),
    )(*args)


def solution(mesh):
    def local(checkpoint, adjoint, line_inverse, row_source):
        rows = checkpoint.shape[1]
        plan = Plan(mesh, rows, line_inverse.shape[1])
        chips = plan.chips

        def run(kernel, outs, *args, flops=None):
            return call(lambda *refs: kernel(plan, *refs), outs, *args, flops=flops)

        def send(part, moves):
            return lax.ppermute(part, AXES, moves)

        def share(edges):
            return ((NC * rows // 2 + edges * plan.edge_rows, LANES), f32)

        full = ((NC, rows, LANES), f32)
        half = ((NC, rows // 2, LANES), f32)
        edge = ((8, rows), f32)
        parts = ((2, chips, NC, plan.part_pad, LANES), f32)
        put_shape, get_shape = ((plan.slots, rows), bf16), ((rows, plan.slots), bf16)
        checkpoint = checkpoint.reshape(full[0])
        adjoint = adjoint.reshape(full[0])
        inverse = line_inverse.reshape(line_inverse.shape[1:])
        source = row_source.reshape(plan.span, rows)
        source = jnp.pad(source, ((0, -plan.span % 8), (0, 0)), constant_values=-1)

        (mine,) = call(pack_kernel, [half], checkpoint)
        state_got = send(mine, plan.swap_x)
        outward, inward, partner, own = run(edge_kernel, [edge] * 4, checkpoint)
        outward_got = send(outward, plan.outward)
        inward_got = send(inward, plan.inward)
        (carried,) = run(carried_kernel, [full], adjoint, inverse)
        put, get = run(slot_kernel, [put_shape, get_shape], source)
        (mine,) = run(share_kernel, [share(2)], carried, partner, inward_got, outward_got)
        share_got = send(mine, plan.swap_x)
        flux, face, *near = run(
            first_kernel,
            [full, parts] + [half] * len(plan.swap_z),
            *(checkpoint, state_got, put),
        )
        crossed = send(face[1], plan.swap_core)
        near_got = [send(part, moves) for part, moves in zip(near, plan.swap_z)]
        face_got = [
            send(jnp.stack([face[0, t], crossed[t]]), plan.swap_face[t]) for t in range(chips)
        ]
        base, pair, tangent, pair_tangent = run(
            local_kernel,
            [full] * 4,
            *(checkpoint, state_got, flux, carried, share_got, outward_got, own),
        )
        core, partial, mine, straight, diag, cross, inward, own = run(
            second_kernel,
            [(parts[0][1:], f32), full, share(1), parts, parts] + [edge] * 3,
            *(base, pair, pair_tangent, get, put, *face_got[::-1], *near_got),
        )
        crossed = send(core, plan.swap_core)
        share_got = send(mine, plan.swap_x)
        z, x, _ = place()
        turned = jnp.logical_xor(x == 0, z == plan.inlet)
        at_face = jnp.logical_or(z == plan.inlet, z == plan.inlet - 1)

        def halo(part, moves, by_face):
            other = jnp.where(by_face, crossed, part[1])
            return [send(jnp.stack([part[0, t], other[t]]), moves[t]) for t in range(chips)]

        straight_got = halo(straight, plan.straight, jnp.logical_and(at_face, turned))
        diag_got = halo(diag, plan.diag, jnp.logical_and(at_face, jnp.logical_not(turned)))
        (cross, inward), _ = lax.optimization_barrier(((cross, inward), diag_got[0]))
        cross_got = send(cross, plan.cross)
        inward_got = send(inward, plan.inward)
        (rest,) = run(rest_kernel, [full], tangent, get, *diag_got, *straight_got[::-1])
        (out,) = run(
            last_kernel,
            [full],
            *(partial, rest, tangent, share_got, cross_got, inward_got, own),
        )
        return out.reshape(NC, rows, 1, LANES)

    return jax.shard_map(
        local,
        mesh=mesh,
        in_specs=(
            P(None, None, "stream", "span"),
            P(None, None, "stream", "span"),
            P("stream", None, None, None),
            P(),
        ),
        out_specs=P(None, None, "stream", "span"),
        check_vma=False,
    )
```

```python
import jax
import jax.numpy as jnp
from jax import lax
from jax.experimental import pallas as pl
from jax.experimental.pallas import tpu as pltpu
from jax.sharding import PartitionSpec as P

time_step = 0.5
ADVECTION = (1.0, 0.6, 0.8, 1.2, 0.7)
DISSIPATION = (0.3, 0.25, 0.35, 0.3, 0.4)
SPREADING = (0.4, 0.3, 0.5, 0.35, 0.45)
NC = 5
LANES = 128
HALF = 64
AXES = ("stream", "span")
f32 = jnp.float32
bf16 = jnp.bfloat16


class Plan:
    def __init__(self, mesh, rows, blocks):
        self.stream = mesh.shape["stream"]
        self.span = mesh.shape["span"]
        self.rows = rows
        self.blocks = blocks
        self.block_rows = rows // blocks
        self.pairs = self.stream // 2
        self.inlet = self.stream // 4
        assert self.stream % 4 == 0 and self.inlet % 2 == 0 and self.span % 2 == 0
        self.chips = self.span // 2
        self.capacity = rows // self.span
        self.part = self.capacity // 2
        self.part_pad = -(-self.part // 8) * 8
        self.packed = self.span * self.part_pad
        self.slots = 2 * self.packed
        self.edge_rows = 8 * -(-rows // LANES)
        zs, js = range(self.pairs), range(self.span)
        self.swap_core = self.full({})
        self.swap_x = self.full(
            {self.at(z, x, j): self.at(z, 1 - x, j) for z in zs for j in js for x in range(2)}
        )
        self.swap_z = []
        for parity in (0, 1):
            moves = {}
            for z in zs[:-1]:
                if z % 2 == parity and z + 1 != self.inlet:
                    for x in range(2):
                        for j in js:
                            self.trade(moves, self.at(z, x, j), self.at(z + 1, x, j))
            if moves:
                self.swap_z.append(self.full(moves))
        self.swap_face, self.straight, self.diag = [], [], []
        for turn in range(self.chips):
            face, straight, diag = {}, {}, {}
            for j in js:
                for z in zs[:-1]:
                    up = down = j
                    if z + 1 == self.inlet:
                        up = (j // 2 + turn) % self.chips * 2 + j % 2
                        down = (j // 2 - turn) % self.chips * 2 + j % 2
                        for x in range(2):
                            self.trade(face, self.at(z, x, j), self.at(z + 1, x, up))
                    straight[self.at(z, 0, j)] = self.at(z + 1, 0, up)
                    straight[self.at(z + 1, 1, j)] = self.at(z, 1, down)
                    self.trade(diag, self.at(z, 1, j), self.at(z + 1, 0, up))
                last = self.pairs - 1
                straight[self.at(last, 0, j)] = self.at(last, 1, j)
                straight[self.at(0, 1, j)] = self.at(0, 0, j)
            self.swap_face.append(self.full(face))
            self.straight.append(self.full(straight))
            self.diag.append(self.full(diag))
        outward, inward, cross = {}, {}, {}
        for z in zs:
            for j in js:
                after, before = (j + 1) % self.span, (j - 1) % self.span
                outward[self.at(z, 0, j)] = self.at(z, 0, after)
                outward[self.at(z, 1, j)] = self.at(z, 1, before)
                inward[self.at(z, 0, j)] = self.at(z, 0, before)
                inward[self.at(z, 1, j)] = self.at(z, 1, after)
                self.trade(cross, self.at(z, 1, j), self.at(z, 0, after))
        self.outward, self.inward, self.cross = map(self.full, (outward, inward, cross))

    def at(self, z, x, j):
        return (2 * z + x) * self.span + j

    def trade(self, moves, a, b):
        moves[a], moves[b] = b, a

    def full(self, moves):
        return [(d, moves.get(d, d ^ 1)) for d in range(self.stream * self.span)]


def place():
    s = lax.axis_index("stream")
    return s // 2, lax.rem(s, 2), lax.axis_index("span")


def is_low(rows):
    return lax.broadcasted_iota(jnp.int32, (rows, LANES), 1) < HALF


def split2(values):
    high = values.astype(bf16)
    return high, (values - high.astype(f32)).astype(bf16)


def dot(a, b, dims=((1,), (0,))):
    return lax.dot_general(a, b, (dims, ((), ())), preferred_element_type=f32)


def permuted(matrix, block):
    both = dot(matrix, jnp.concatenate(split2(block), axis=1))
    return both[:, :LANES] + both[:, LANES:]


def half_turn(block):
    return pltpu.roll(block, HALF, 1)


def pack(block, high):
    rows = block.shape[0] // 2
    return jnp.where(
        is_low(rows),
        pltpu.roll(block[:rows], HALF * high, 1),
        pltpu.roll(block[rows:], HALF * (1 - high), 1),
    )


def unpack(packed, high):
    return jnp.concatenate(
        [pltpu.roll(packed, HALF * high, 1), pltpu.roll(packed, HALF * (1 - high), 1)], axis=0
    )


def unpack2(for_low, for_high):
    low = is_low(for_low.shape[0])
    return jnp.concatenate(
        [
            jnp.where(low, for_low, half_turn(for_high)),
            jnp.where(low, half_turn(for_low), for_high),
        ],
        axis=0,
    )


def padded(plan, half):
    gap = plan.packed - half.shape[0]
    return jnp.concatenate([half, jnp.zeros((gap, LANES), f32)], axis=0) if gap else half


def spread(plan, block):
    half = plan.rows // 2
    if plan.packed == half:
        return block
    return jnp.concatenate([padded(plan, block[:half]), padded(plan, block[half:])], axis=0)


def gathered(plan, slots):
    half = plan.rows // 2
    if plan.packed == half:
        return slots
    return jnp.concatenate([slots[:half], slots[plan.packed : plan.packed + half]], axis=0)


def pairing(plan, own, arrived, x):
    return jnp.where(jnp.logical_xor(is_low(plan.rows), x == 1), own, unpack(arrived, 1 - x))


def picks(lanes):
    shape = (8 * len(lanes), NC * LANES)
    row = lax.broadcasted_iota(jnp.int32, shape, 0)
    lane = lax.broadcasted_iota(jnp.int32, shape, 1)
    hit = row < 0
    for i, at in enumerate(lanes):
        for c in range(NC):
            hit = hit | ((row == 8 * i + c) & (lane == c * LANES + at))
    return jnp.where(hit, 1.0, 0.0).astype(bf16)


def edges_of(blocks, lanes):
    blocks = jnp.concatenate([block.astype(bf16) for block in blocks], axis=1)
    return dot(picks(lanes), blocks, ((1,), (1,)))


def edges_at(edges, lanes):
    return dot(edges.astype(bf16), picks(lanes), ((0,), (0,)))


def put_edge(plan, out_ref, i, edge):
    at = NC * plan.rows // 2 + i * plan.edge_rows
    for start in range(0, plan.rows, LANES):
        width = min(LANES, plan.rows - start)
        out_ref[at : at + 8, :width] = edge[:, start : start + width]
        if width < LANES:
            out_ref[at : at + 8, width:] = jnp.zeros((8, LANES - width), f32)
        at += 8


def get_edge(plan, ref, i):
    at = NC * plan.rows // 2 + i * plan.edge_rows
    parts = []
    for start in range(0, plan.rows, LANES):
        parts.append(ref[at : at + 8, : min(LANES, plan.rows - start)])
        at += 8
    return jnp.concatenate(parts, axis=1)


def lane_row(values):
    lane = lax.broadcasted_iota(jnp.int32, (1, LANES), 1)
    row = jnp.zeros((1, LANES), f32)
    for hit, value in values(lane):
        row = jnp.where(hit, value, row)
    return row


def lateral(block):
    inner_left = lane_row(lambda lane: [((lane & (HALF - 1)) != 0, 1.0)])
    inner_right = lane_row(lambda lane: [((lane & (HALF - 1)) != HALF - 1, 1.0)])
    left = pltpu.roll(block, 1, 1) * inner_left
    right = pltpu.roll(block, LANES - 1, 1) * inner_right
    return left + right - 2.0 * block


def halves(low, high):
    return lane_row(lambda lane: [(lane < HALF, low), (lane >= HALF, high)])


def coefficients(c):
    down = -0.5 * ADVECTION[c] + DISSIPATION[c]
    up = 0.5 * ADVECTION[c] + DISSIPATION[c]
    return down, up


def pack_kernel(block_ref, out_ref):
    _, x, _ = place()
    for c in range(NC):
        out_ref[c] = pack(block_ref[c], 1 - x)


def slot_kernel(plan, source_ref, put_ref, get_ref):
    rows, span, chips = plan.rows, plan.span, plan.chips
    z, _, j = place()
    source = [source_ref[:, d * rows : (d + 1) * rows] for d in range(span)]
    source += [jnp.full((1, rows), -1, jnp.int32)] * (-span % 8)
    source = jnp.concatenate(source, axis=0)
    own_chip, own_core = j // 2, lax.rem(j, 2)

    def order(other, sign):
        core = jnp.where(other % 2 == own_core, 0, 1)
        turn = lax.rem(sign * (other // 2 - own_chip) + chips, chips)
        return ((core * chips + turn) * plan.part_pad).astype(f32)

    sub = lax.broadcasted_iota(jnp.int32, (rows, rows), 0)
    lane = lax.broadcasted_iota(jnp.int32, (rows, rows), 1)
    before = jnp.where(sub < lane, 1.0, 0.0).astype(bf16)
    arrival = jnp.zeros(source.shape, f32)
    base = jnp.zeros(source.shape, f32)
    for d in range(span):
        here = jnp.where((source >= d * rows) & (source < (d + 1) * rows), 1.0, 0.0)
        arrival += here * dot(here.astype(bf16), before)
        base += here * order(d, -1)
    late = jnp.where(arrival >= plan.part, 1.0, 0.0)
    within = arrival + late * (plan.packed - plan.part)
    own = lax.broadcasted_iota(jnp.int32, source.shape, 0) == j
    stator_row = jnp.sum(jnp.where(own, base + within, 0.0), axis=0, keepdims=True)
    total = jnp.zeros((rows, rows), f32)
    for d in range(span):
        match = source[d : d + 1] - j * rows == sub
        total += jnp.where(match, within[d : d + 1] + order(d, 1), 0.0)
    rotor_col = jnp.sum(total, axis=1, keepdims=True)
    same = sub == lane
    stator_col = jnp.sum(jnp.where(same, stator_row, 0.0), axis=1, keepdims=True)
    rotor_row = jnp.sum(jnp.where(same, rotor_col, 0.0), axis=0, keepdims=True)
    stator = z == plan.inlet
    col = jnp.where(stator, stator_col, rotor_col).astype(jnp.int32)
    row = jnp.where(stator, stator_row, rotor_row).astype(jnp.int32)
    put = lax.broadcasted_iota(jnp.int32, (plan.slots, rows), 0) == row
    get = lax.broadcasted_iota(jnp.int32, (rows, plan.slots), 1) == col
    put_ref[...] = jnp.where(put, 1.0, 0.0).astype(bf16)
    get = jnp.logical_and(get, jnp.logical_or(stator, z == plan.inlet - 1))
    get_ref[...] = jnp.where(get, 1.0, 0.0).astype(bf16)


def carried_kernel(plan, adjoint_ref, inverse_ref, carried_ref):
    size = plan.block_rows
    for b in range(plan.blocks):
        rounded = jnp.concatenate(
            [adjoint_ref[c, b * size : (b + 1) * size].astype(bf16) for c in range(NC)], axis=0
        )
        product = dot(inverse_ref[b], rounded, ((0,), (0,)))
        for c in range(NC):
            carried_ref[c, b * size : (b + 1) * size] = product[c * size : (c + 1) * size]


def edge_kernel(plan, block_ref, outward_ref, inward_ref, partner_ref, own_ref):
    _, x, _ = place()
    blocks = [jnp.tanh(block_ref[c]) for c in range(NC)]
    edges = edges_of(blocks, [127 * (1 - x), 127 * x, 63 + x, 64 - x])
    for i, ref in enumerate((outward_ref, inward_ref, partner_ref, own_ref)):
        ref[...] = edges[8 * i : 8 * i + 8]


def share_kernel(plan, carried_ref, partner_ref, inward_ref, *refs):
    out_ref = refs[-1]
    _, x, _ = place()
    half = plan.rows // 2
    for c in range(NC):
        out_ref[c * half : (c + 1) * half] = pack(carried_ref[c], 1 - x)
    put_edge(plan, out_ref, 0, partner_ref[...])
    put_edge(plan, out_ref, 1, inward_ref[...])


def in_slots(plan, block, put):
    z, _, _ = place()
    low = is_low(plan.slots)
    face = jnp.logical_or(
        jnp.logical_and(low, z == plan.inlet),
        jnp.logical_and(jnp.logical_not(low), z == plan.inlet - 1),
    )
    return jnp.where(face, permuted(put, block), spread(plan, block))


def sending(plan, slots):
    turned = half_turn(slots)
    low, n = is_low(plan.packed), plan.packed
    to_before = jnp.where(low, slots[:n], turned[n:])
    to_after = jnp.where(low, turned[:n], slots[n:])
    return to_before, to_after


def put_parts(plan, ref, c, packed):
    for core in range(2):
        for turn in range(plan.chips):
            at = (core * plan.chips + turn) * plan.part_pad
            ref[core, turn, c] = packed[at : at + plan.part_pad]


def get_parts(plan, refs, c):
    parts = [refs[t][core, c] for core in range(2) for t in range(plan.chips)]
    return jnp.concatenate(parts, axis=0)


def first_kernel(plan, block_ref, arrived_ref, put_ref, flux_ref, face_ref, *z_refs):
    z, x, _ = place()
    odd = lax.rem(z, 2) == 1
    put = put_ref[...]
    half = plan.rows // 2
    for c in range(NC):
        flux = jnp.tanh(pairing(plan, block_ref[c], arrived_ref[c], x))
        flux_ref[c] = flux
        to_before, to_after = sending(plan, in_slots(plan, flux, put))
        swap = jnp.where(odd, to_before, to_after)
        other = jnp.where(odd, to_after, to_before)
        z_refs[0][c] = swap[:half]
        if len(z_refs) > 1:
            z_refs[1][c] = other[:half]
        put_parts(plan, face_ref, c, other)


def local_kernel(
    plan, block_ref, arrived_ref, flux_ref, carried_ref, share_ref, *refs
):
    outward_ref, own_ref, base_ref, pair_ref, tangent_ref, pair_tangent_ref = refs
    _, x, _ = place()
    half = plan.rows // 2
    low = is_low(plan.rows)
    forwarded, partner = get_edge(plan, share_ref, 1), get_edge(plan, share_ref, 0)
    edges = jnp.concatenate([outward_ref[...], forwarded, partner, own_ref[...]], axis=0)
    ghosts = edges_at(edges, [127 * x, 64 - x, 127 * (1 - x), 63 + x])
    for c in range(NC):
        own, flux = block_ref[c], flux_ref[c]
        state = pairing(plan, own, arrived_ref[c], x)
        down, up = coefficients(c)
        ghost = ghosts[:, c * LANES : (c + 1) * LANES]
        change = (
            halves(down, up) * half_turn(flux)
            - 2.0 * DISSIPATION[c] * flux
            + SPREADING[c] * (lateral(flux) + ghost)
        )
        base_ref[c] = state + time_step * change
        pair_tangent_ref[c] = time_step * (1.0 - flux * flux)
        share = share_ref[c * half : (c + 1) * half]
        pair_ref[c] = pairing(plan, carried_ref[c], share, x)
        flux = jnp.tanh(own)
        tangent_ref[c] = time_step * (1.0 - flux * flux)


def second_kernel(plan, base_ref, pair_ref, tangent_ref, get_ref, put_ref, *refs):
    chips, count = plan.chips, len(plan.swap_z)
    face_refs, z_refs = refs[:chips][::-1], refs[chips : chips + count]
    core_ref, partial_ref, out_ref, straight_ref, diag_ref, *edge_refs = refs[chips + count :]
    z, x, _ = place()
    odd = lax.rem(z, 2) == 1
    low = is_low(plan.rows)
    swapped = jnp.logical_xor(low, jnp.logical_not(odd))
    at_face = jnp.logical_or(z == plan.inlet, z == plan.inlet - 1)
    at_end = jnp.logical_or(z == 0, z == plan.pairs - 1)
    put, get = put_ref[...], get_ref[...]
    half = plan.rows // 2
    blocks = []
    for c in range(NC):
        face = get_parts(plan, face_refs, c)
        near = padded(plan, z_refs[0][c])
        slots = unpack2(jnp.where(odd, near, face), jnp.where(odd, face, near))
        moved = permuted(get, slots)
        if count > 1:
            far = padded(plan, z_refs[1][c])
            slots = unpack2(jnp.where(odd, near, far), jnp.where(odd, far, near))
            far = jnp.where(jnp.logical_or(at_face, at_end), moved, gathered(plan, slots))
        else:
            far = moved
        halo = jnp.where(swapped, gathered(plan, slots), far)
        down, up = coefficients(c)
        slope = jnp.tanh(base_ref[c] + halves(time_step * up, time_step * down) * halo)
        weighted = (2.0 - slope * slope) * pair_ref[c]
        change = (
            halves(up, down) * half_turn(weighted)
            - 2.0 * DISSIPATION[c] * weighted
            + SPREADING[c] * lateral(weighted)
        )
        partial = weighted + tangent_ref[c] * change
        partial_ref[c] = partial
        out_ref[c * half : (c + 1) * half] = pack(partial, 1 - x)
        to_before, to_after = sending(plan, in_slots(plan, weighted, put))
        put_parts(plan, straight_ref, c, jnp.where(x == 0, to_after, to_before))
        put_parts(plan, diag_ref, c, jnp.where(x == 0, to_before, to_after))
        face = jnp.where(z < plan.inlet, to_after, to_before)
        for turn in range(chips):
            at = (chips + turn) * plan.part_pad
            core_ref[turn, c] = face[at : at + plan.part_pad]
        blocks.append(weighted)
    edges = edges_of(blocks, [127 * (1 - x), 64 - x, 127 * x, 63 + x])
    put_edge(plan, out_ref, 0, edges[:8])
    for i, ref in enumerate(edge_refs):
        ref[...] = edges[8 * i + 8 : 8 * i + 16]


def rest_kernel(plan, tangent_ref, get_ref, *refs):
    chips = plan.chips
    diag_refs, straight_refs, rest_ref = refs[:chips], refs[chips : 2 * chips][::-1], refs[2 * chips]
    z, x, _ = place()
    first = x == 0
    at_face = z == jnp.where(first, plan.inlet, plan.inlet - 1)
    at_end = z == jnp.where(first, 0, plan.pairs - 1)
    get = get_ref[...]
    for c in range(NC):
        straight = get_parts(plan, straight_refs, c)
        diag = get_parts(plan, diag_refs, c)
        slots = unpack2(jnp.where(first, straight, diag), jnp.where(first, diag, straight))
        moved = permuted(get, slots)
        halo = jnp.where(at_face, moved, jnp.where(at_end, 0.0, gathered(plan, slots)))
        down, up = coefficients(c)
        rest_ref[c] = tangent_ref[c] * (jnp.where(first, down, up) * halo)


def last_kernel(plan, partial_ref, rest_ref, tangent_ref, share_ref, *refs):
    cross_ref, inward_ref, own_ref, out_ref = refs
    _, x, _ = place()
    half = plan.rows // 2
    edges = [get_edge(plan, share_ref, 0), cross_ref[...], inward_ref[...], own_ref[...]]
    ghosts = edges_at(
        jnp.concatenate(edges, axis=0), [63 + x, 127 * x, 127 * (1 - x), 64 - x]
    )
    for c in range(NC):
        ghost = ghosts[:, c * LANES : (c + 1) * LANES]
        share = share_ref[c * half : (c + 1) * half]
        rest = rest_ref[c] + tangent_ref[c] * (SPREADING[c] * ghost)
        out_ref[c] = pairing(plan, partial_ref[c], share, x) + rest


def call(kernel, outs, *args, flops=None):
    whole = pl.BlockSpec(memory_space=pltpu.VMEM)
    return pl.pallas_call(
        kernel,
        out_shape=[jax.ShapeDtypeStruct(shape, dtype) for shape, dtype in outs],
        in_specs=[whole] * len(args),
        out_specs=[whole] * len(outs),
        compiler_params=pltpu.CompilerParams(vmem_limit_bytes=16 * 2**20),
        cost_estimate=flops
        and pl.CostEstimate(flops=flops, bytes_accessed=0, transcendentals=0),
    )(*args)


def solution(mesh):
    def local(checkpoint, adjoint, line_inverse, row_source):
        rows = checkpoint.shape[1]
        plan = Plan(mesh, rows, line_inverse.shape[1])
        chips = plan.chips

        def run(kernel, outs, *args, flops=None):
            return call(lambda *refs: kernel(plan, *refs), outs, *args, flops=flops)

        def send(part, moves):
            return lax.ppermute(part, AXES, moves)

        def share(edges):
            return ((NC * rows // 2 + edges * plan.edge_rows, LANES), f32)

        full = ((NC, rows, LANES), f32)
        half = ((NC, rows // 2, LANES), f32)
        edge = ((8, rows), f32)
        parts = ((2, chips, NC, plan.part_pad, LANES), f32)
        put_shape, get_shape = ((plan.slots, rows), bf16), ((rows, plan.slots), bf16)
        checkpoint = checkpoint.reshape(full[0])
        adjoint = adjoint.reshape(full[0])
        inverse = line_inverse.reshape(line_inverse.shape[1:])
        source = row_source.reshape(1, plan.span * rows)

        (mine,) = call(pack_kernel, [half], checkpoint)
        state_got = send(mine, plan.swap_x)
        outward, inward, partner, own = run(edge_kernel, [edge] * 4, checkpoint)
        outward_got = send(outward, plan.outward)
        inward_got = send(inward, plan.inward)
        (carried,) = run(carried_kernel, [full], adjoint, inverse)
        put, get = run(slot_kernel, [put_shape, get_shape], source)
        (mine,) = run(share_kernel, [share(2)], carried, partner, inward_got, outward_got)
        share_got = send(mine, plan.swap_x)
        flux, face, *near = run(
            first_kernel,
            [full, parts] + [half] * len(plan.swap_z),
            *(checkpoint, state_got, put),
        )
        crossed = send(face[1], plan.swap_core)
        near_got = [send(part, moves) for part, moves in zip(near, plan.swap_z)]
        face_got = [
            send(jnp.stack([face[0, t], crossed[t]]), plan.swap_face[t]) for t in range(chips)
        ]
        base, pair, tangent, pair_tangent = run(
            local_kernel,
            [full] * 4,
            *(checkpoint, state_got, flux, carried, share_got, outward_got, own),
        )
        core, partial, mine, straight, diag, cross, inward, own = run(
            second_kernel,
            [(parts[0][1:], f32), full, share(1), parts, parts] + [edge] * 3,
            *(base, pair, pair_tangent, get, put, *face_got[::-1], *near_got),
        )
        crossed = send(core, plan.swap_core)
        share_got = send(mine, plan.swap_x)
        z, x, _ = place()
        turned = jnp.logical_xor(x == 0, z == plan.inlet)
        at_face = jnp.logical_or(z == plan.inlet, z == plan.inlet - 1)

        def halo(part, moves, by_face):
            other = jnp.where(by_face, crossed, part[1])
            return [send(jnp.stack([part[0, t], other[t]]), moves[t]) for t in range(chips)]

        straight_got = halo(straight, plan.straight, jnp.logical_and(at_face, turned))
        diag_got = halo(diag, plan.diag, jnp.logical_and(at_face, jnp.logical_not(turned)))
        (cross, inward), _ = lax.optimization_barrier(((cross, inward), diag_got[0]))
        cross_got = send(cross, plan.cross)
        inward_got = send(inward, plan.inward)
        (rest,) = run(rest_kernel, [full], tangent, get, *diag_got, *straight_got[::-1])
        (out,) = run(
            last_kernel,
            [full],
            *(partial, rest, tangent, share_got, cross_got, inward_got, own),
        )
        return out.reshape(NC, rows, 1, LANES)

    return jax.shard_map(
        local,
        mesh=mesh,
        in_specs=(
            P(None, None, "stream", "span"),
            P(None, None, "stream", "span"),
            P("stream", None, None, None),
            P(),
        ),
        out_specs=P(None, None, "stream", "span"),
        check_vma=False,
    )
```

```python
import jax
import jax.numpy as jnp
from jax import lax
from jax.experimental import pallas as pl
from jax.experimental.pallas import tpu as pltpu
from jax.sharding import PartitionSpec as P

time_step = 0.5
ADVECTION = (1.0, 0.6, 0.8, 1.2, 0.7)
DISSIPATION = (0.3, 0.25, 0.35, 0.3, 0.4)
SPREADING = (0.4, 0.3, 0.5, 0.35, 0.45)
NC = 5
LANES = 128
HALF = 64
AXES = ("stream", "span")
f32 = jnp.float32
bf16 = jnp.bfloat16


class Plan:
    def __init__(self, mesh, rows, blocks):
        self.stream = mesh.shape["stream"]
        self.span = mesh.shape["span"]
        self.rows = rows
        self.blocks = blocks
        self.block_rows = rows // blocks
        self.pairs = self.stream // 2
        self.inlet = self.stream // 4
        assert self.stream % 4 == 0 and self.inlet % 2 == 0 and self.span % 2 == 0
        self.chips = self.span // 2
        self.capacity = rows // self.span
        self.part = self.capacity // 2
        self.part_pad = -(-self.part // 8) * 8
        self.packed = self.span * self.part_pad
        self.slots = 2 * self.packed
        self.edge_rows = 8 * -(-rows // LANES)
        zs, js = range(self.pairs), range(self.span)
        self.swap_core = self.full({})
        self.swap_x = self.full(
            {self.at(z, x, j): self.at(z, 1 - x, j) for z in zs for j in js for x in range(2)}
        )
        self.swap_z = []
        for parity in (0, 1):
            moves = {}
            for z in zs[:-1]:
                if z % 2 == parity and z + 1 != self.inlet:
                    for x in range(2):
                        for j in js:
                            self.trade(moves, self.at(z, x, j), self.at(z + 1, x, j))
            if moves:
                self.swap_z.append(self.full(moves))
        self.swap_face, self.straight, self.diag = [], [], []
        for turn in range(self.chips):
            face, straight, diag = {}, {}, {}
            for j in js:
                for z in zs[:-1]:
                    up = down = j
                    if z + 1 == self.inlet:
                        up = (j // 2 + turn) % self.chips * 2 + j % 2
                        down = (j // 2 - turn) % self.chips * 2 + j % 2
                        for x in range(2):
                            self.trade(face, self.at(z, x, j), self.at(z + 1, x, up))
                    straight[self.at(z, 0, j)] = self.at(z + 1, 0, up)
                    straight[self.at(z + 1, 1, j)] = self.at(z, 1, down)
                    self.trade(diag, self.at(z, 1, j), self.at(z + 1, 0, up))
                last = self.pairs - 1
                straight[self.at(last, 0, j)] = self.at(last, 1, j)
                straight[self.at(0, 1, j)] = self.at(0, 0, j)
            self.swap_face.append(self.full(face))
            self.straight.append(self.full(straight))
            self.diag.append(self.full(diag))
        outward, inward, cross = {}, {}, {}
        for z in zs:
            for j in js:
                after, before = (j + 1) % self.span, (j - 1) % self.span
                outward[self.at(z, 0, j)] = self.at(z, 0, after)
                outward[self.at(z, 1, j)] = self.at(z, 1, before)
                inward[self.at(z, 0, j)] = self.at(z, 0, before)
                inward[self.at(z, 1, j)] = self.at(z, 1, after)
                self.trade(cross, self.at(z, 1, j), self.at(z, 0, after))
        self.outward, self.inward, self.cross = map(self.full, (outward, inward, cross))

    def at(self, z, x, j):
        return (2 * z + x) * self.span + j

    def trade(self, moves, a, b):
        moves[a], moves[b] = b, a

    def full(self, moves):
        return [(d, moves.get(d, d ^ 1)) for d in range(self.stream * self.span)]


def place():
    s = lax.axis_index("stream")
    return s // 2, lax.rem(s, 2), lax.axis_index("span")


def is_low(rows):
    return lax.broadcasted_iota(jnp.int32, (rows, LANES), 1) < HALF


def split2(values):
    high = values.astype(bf16)
    return high, (values - high.astype(f32)).astype(bf16)


def dot(a, b, dims=((1,), (0,))):
    return lax.dot_general(a, b, (dims, ((), ())), preferred_element_type=f32)


def permuted(matrix, block):
    both = dot(matrix, jnp.concatenate(split2(block), axis=1))
    return both[:, :LANES] + both[:, LANES:]


def half_turn(block):
    return pltpu.roll(block, HALF, 1)


def pack(block, high):
    rows = block.shape[0] // 2
    return jnp.where(
        is_low(rows),
        pltpu.roll(block[:rows], HALF * high, 1),
        pltpu.roll(block[rows:], HALF * (1 - high), 1),
    )


def unpack(packed, high):
    return jnp.concatenate(
        [pltpu.roll(packed, HALF * high, 1), pltpu.roll(packed, HALF * (1 - high), 1)], axis=0
    )


def unpack2(for_low, for_high):
    low = is_low(for_low.shape[0])
    return jnp.concatenate(
        [
            jnp.where(low, for_low, half_turn(for_high)),
            jnp.where(low, half_turn(for_low), for_high),
        ],
        axis=0,
    )


def padded(plan, half):
    gap = plan.packed - half.shape[0]
    return jnp.concatenate([half, jnp.zeros((gap, LANES), f32)], axis=0) if gap else half


def spread(plan, block):
    half = plan.rows // 2
    if plan.packed == half:
        return block
    return jnp.concatenate([padded(plan, block[:half]), padded(plan, block[half:])], axis=0)


def gathered(plan, slots):
    half = plan.rows // 2
    if plan.packed == half:
        return slots
    return jnp.concatenate([slots[:half], slots[plan.packed : plan.packed + half]], axis=0)


def pairing(plan, own, arrived, x):
    return jnp.where(jnp.logical_xor(is_low(plan.rows), x == 1), own, unpack(arrived, 1 - x))


def picks(lanes):
    shape = (8 * len(lanes), NC * LANES)
    row = lax.broadcasted_iota(jnp.int32, shape, 0)
    lane = lax.broadcasted_iota(jnp.int32, shape, 1)
    hit = row < 0
    for i, at in enumerate(lanes):
        for c in range(NC):
            hit = hit | ((row == 8 * i + c) & (lane == c * LANES + at))
    return jnp.where(hit, 1.0, 0.0).astype(bf16)


def edge_of(c, block, lanes):
    chosen = picks(lanes)[:, c * LANES : (c + 1) * LANES]
    return dot(chosen, block.astype(bf16), ((1,), (1,)))


def edges_of(blocks, lanes):
    blocks = jnp.concatenate([block.astype(bf16) for block in blocks], axis=1)
    return dot(picks(lanes), blocks, ((1,), (1,)))


def edges_at(edges, lanes):
    return dot(edges.astype(bf16), picks(lanes), ((0,), (0,)))


def put_edge(plan, out_ref, i, edge):
    at = NC * plan.rows // 2 + i * plan.edge_rows
    for start in range(0, plan.rows, LANES):
        width = min(LANES, plan.rows - start)
        out_ref[at : at + 8, :width] = edge[:, start : start + width]
        if width < LANES:
            out_ref[at : at + 8, width:] = jnp.zeros((8, LANES - width), f32)
        at += 8


def get_edge(plan, ref, i):
    at = NC * plan.rows // 2 + i * plan.edge_rows
    parts = []
    for start in range(0, plan.rows, LANES):
        parts.append(ref[at : at + 8, : min(LANES, plan.rows - start)])
        at += 8
    return jnp.concatenate(parts, axis=1)


def lane_row(values):
    lane = lax.broadcasted_iota(jnp.int32, (1, LANES), 1)
    row = jnp.zeros((1, LANES), f32)
    for hit, value in values(lane):
        row = jnp.where(hit, value, row)
    return row


def lateral(block):
    inner_left = lane_row(lambda lane: [((lane & (HALF - 1)) != 0, 1.0)])
    inner_right = lane_row(lambda lane: [((lane & (HALF - 1)) != HALF - 1, 1.0)])
    left = pltpu.roll(block, 1, 1) * inner_left
    right = pltpu.roll(block, LANES - 1, 1) * inner_right
    return left + right - 2.0 * block


def halves(low, high):
    return lane_row(lambda lane: [(lane < HALF, low), (lane >= HALF, high)])


def coefficients(c):
    down = -0.5 * ADVECTION[c] + DISSIPATION[c]
    up = 0.5 * ADVECTION[c] + DISSIPATION[c]
    return down, up


def pack_kernel(block_ref, out_ref):
    _, x, _ = place()
    for c in range(NC):
        out_ref[c] = pack(block_ref[c], 1 - x)


def slot_kernel(plan, source_ref, put_ref, get_ref):
    rows, span, chips = plan.rows, plan.span, plan.chips
    z, _, j = place()
    source = source_ref[...]
    own_chip, own_core = j // 2, lax.rem(j, 2)

    def order(other, sign):
        core = jnp.where(other % 2 == own_core, 0, 1)
        turn = lax.rem(sign * (other // 2 - own_chip) + chips, chips)
        return ((core * chips + turn) * plan.part_pad).astype(f32)

    sub = lax.broadcasted_iota(jnp.int32, (rows, rows), 0)
    lane = lax.broadcasted_iota(jnp.int32, (rows, rows), 1)
    before = jnp.where(sub < lane, 1.0, 0.0).astype(bf16)
    arrival = jnp.zeros(source.shape, f32)
    base = jnp.zeros(source.shape, f32)
    for d in range(span):
        here = jnp.where((source >= d * rows) & (source < (d + 1) * rows), 1.0, 0.0)
        arrival += here * dot(here.astype(bf16), before)
        base += here * order(d, -1)
    late = jnp.where(arrival >= plan.part, 1.0, 0.0)
    within = arrival + late * (plan.packed - plan.part)
    own = lax.broadcasted_iota(jnp.int32, source.shape, 0) == j
    stator_row = jnp.sum(jnp.where(own, base + within, 0.0), axis=0, keepdims=True)
    total = jnp.zeros((rows, rows), f32)
    for d in range(span):
        match = source[d : d + 1] - j * rows == sub
        total += jnp.where(match, within[d : d + 1] + order(d, 1), 0.0)
    rotor_col = jnp.sum(total, axis=1, keepdims=True)
    same = sub == lane
    stator_col = jnp.sum(jnp.where(same, stator_row, 0.0), axis=1, keepdims=True)
    rotor_row = jnp.sum(jnp.where(same, rotor_col, 0.0), axis=0, keepdims=True)
    stator = z == plan.inlet
    col = jnp.where(stator, stator_col, rotor_col).astype(jnp.int32)
    row = jnp.where(stator, stator_row, rotor_row).astype(jnp.int32)
    put = lax.broadcasted_iota(jnp.int32, (plan.slots, rows), 0) == row
    get = lax.broadcasted_iota(jnp.int32, (rows, plan.slots), 1) == col
    put_ref[...] = jnp.where(put, 1.0, 0.0).astype(bf16)
    get = jnp.logical_and(get, jnp.logical_or(stator, z == plan.inlet - 1))
    get_ref[...] = jnp.where(get, 1.0, 0.0).astype(bf16)


def carried_kernel(plan, adjoint_ref, inverse_ref, carried_ref):
    size = plan.block_rows
    for b in range(plan.blocks):
        rounded = jnp.concatenate(
            [adjoint_ref[c, b * size : (b + 1) * size].astype(bf16) for c in range(NC)], axis=0
        )
        product = dot(inverse_ref[b], rounded, ((0,), (0,)))
        for c in range(NC):
            carried_ref[c, b * size : (b + 1) * size] = product[c * size : (c + 1) * size]


def edge_kernel(plan, block_ref, outward_ref, inward_ref, partner_ref, own_ref):
    _, x, _ = place()
    blocks = [jnp.tanh(block_ref[c]) for c in range(NC)]
    edges = edges_of(blocks, [127 * (1 - x), 127 * x, 63 + x, 64 - x])
    for i, ref in enumerate((outward_ref, inward_ref, partner_ref, own_ref)):
        ref[...] = edges[8 * i : 8 * i + 8]


def share_kernel(plan, carried_ref, partner_ref, inward_ref, *refs):
    out_ref = refs[-1]
    _, x, _ = place()
    half = plan.rows // 2
    for c in range(NC):
        out_ref[c * half : (c + 1) * half] = pack(carried_ref[c], 1 - x)
    put_edge(plan, out_ref, 0, partner_ref[...])
    put_edge(plan, out_ref, 1, inward_ref[...])


def in_slots(plan, block, put):
    z, _, _ = place()
    low = is_low(plan.slots)
    face = jnp.logical_or(
        jnp.logical_and(low, z == plan.inlet),
        jnp.logical_and(jnp.logical_not(low), z == plan.inlet - 1),
    )
    return jnp.where(face, permuted(put, block), spread(plan, block))


def sending(plan, slots):
    turned = half_turn(slots)
    low, n = is_low(plan.packed), plan.packed
    to_before = jnp.where(low, slots[:n], turned[n:])
    to_after = jnp.where(low, turned[:n], slots[n:])
    return to_before, to_after


def put_parts(plan, ref, c, packed):
    for core in range(2):
        for turn in range(plan.chips):
            at = (core * plan.chips + turn) * plan.part_pad
            ref[core, turn, c] = packed[at : at + plan.part_pad]


def get_parts(plan, refs, c):
    parts = [refs[t][core, c] for core in range(2) for t in range(plan.chips)]
    return jnp.concatenate(parts, axis=0)


def first_kernel(plan, block_ref, arrived_ref, put_ref, flux_ref, face_ref, *z_refs):
    z, x, _ = place()
    odd = lax.rem(z, 2) == 1
    put = put_ref[...]
    half = plan.rows // 2
    for c in range(NC):
        flux = jnp.tanh(pairing(plan, block_ref[c], arrived_ref[c], x))
        flux_ref[c] = flux
        to_before, to_after = sending(plan, in_slots(plan, flux, put))
        swap = jnp.where(odd, to_before, to_after)
        other = jnp.where(odd, to_after, to_before)
        z_refs[0][c] = swap[:half]
        if len(z_refs) > 1:
            z_refs[1][c] = other[:half]
        put_parts(plan, face_ref, c, other)


def local_kernel(
    plan, block_ref, arrived_ref, flux_ref, carried_ref, share_ref, *refs
):
    outward_ref, own_ref, base_ref, pair_ref, tangent_ref, pair_tangent_ref = refs
    _, x, _ = place()
    half = plan.rows // 2
    low = is_low(plan.rows)
    forwarded, partner = get_edge(plan, share_ref, 1), get_edge(plan, share_ref, 0)
    edges = jnp.concatenate([outward_ref[...], forwarded, partner, own_ref[...]], axis=0)
    ghosts = edges_at(edges, [127 * x, 64 - x, 127 * (1 - x), 63 + x])
    for c in range(NC):
        own, flux = block_ref[c], flux_ref[c]
        state = pairing(plan, own, arrived_ref[c], x)
        down, up = coefficients(c)
        ghost = ghosts[:, c * LANES : (c + 1) * LANES]
        change = (
            halves(down, up) * half_turn(flux)
            - 2.0 * DISSIPATION[c] * flux
            + SPREADING[c] * (lateral(flux) + ghost)
        )
        base_ref[c] = state + time_step * change
        pair_tangent_ref[c] = time_step * (1.0 - flux * flux)
        share = share_ref[c * half : (c + 1) * half]
        pair_ref[c] = pairing(plan, carried_ref[c], share, x)
        flux = jnp.tanh(own)
        tangent_ref[c] = time_step * (1.0 - flux * flux)


def second_kernel(plan, base_ref, pair_ref, tangent_ref, get_ref, put_ref, *refs):
    chips, count = plan.chips, len(plan.swap_z)
    face_refs, z_refs = refs[:chips][::-1], refs[chips : chips + count]
    core_ref, partial_ref, out_ref, straight_ref, diag_ref, weighted_ref = refs[chips + count :]
    z, x, _ = place()
    odd = lax.rem(z, 2) == 1
    low = is_low(plan.rows)
    swapped = jnp.logical_xor(low, jnp.logical_not(odd))
    at_face = jnp.logical_or(z == plan.inlet, z == plan.inlet - 1)
    at_end = jnp.logical_or(z == 0, z == plan.pairs - 1)
    put, get = put_ref[...], get_ref[...]
    half = plan.rows // 2
    edge = jnp.zeros((8, plan.rows), f32)
    for c in range(NC):
        face = get_parts(plan, face_refs, c)
        near = padded(plan, z_refs[0][c])
        slots = unpack2(jnp.where(odd, near, face), jnp.where(odd, face, near))
        moved = permuted(get, slots)
        if count > 1:
            far = padded(plan, z_refs[1][c])
            slots = unpack2(jnp.where(odd, near, far), jnp.where(odd, far, near))
            far = jnp.where(jnp.logical_or(at_face, at_end), moved, gathered(plan, slots))
        else:
            far = moved
        halo = jnp.where(swapped, gathered(plan, slots), far)
        down, up = coefficients(c)
        slope = jnp.tanh(base_ref[c] + halves(time_step * up, time_step * down) * halo)
        weighted = (2.0 - slope * slope) * pair_ref[c]
        change = (
            halves(up, down) * half_turn(weighted)
            - 2.0 * DISSIPATION[c] * weighted
            + SPREADING[c] * lateral(weighted)
        )
        partial = weighted + tangent_ref[c] * change
        partial_ref[c] = partial
        out_ref[c * half : (c + 1) * half] = pack(partial, 1 - x)
        to_before, to_after = sending(plan, in_slots(plan, weighted, put))
        put_parts(plan, straight_ref, c, jnp.where(x == 0, to_after, to_before))
        put_parts(plan, diag_ref, c, jnp.where(x == 0, to_before, to_after))
        face = jnp.where(z < plan.inlet, to_after, to_before)
        for turn in range(chips):
            at = (chips + turn) * plan.part_pad
            core_ref[turn, c] = face[at : at + plan.part_pad]
        weighted_ref[c] = weighted
        edge += edge_of(c, weighted, [127 * (1 - x)])
    put_edge(plan, out_ref, 0, edge)


def edge2_kernel(plan, weighted_ref, cross_ref, inward_ref, own_ref):
    _, x, _ = place()
    edges = edges_of([weighted_ref[c] for c in range(NC)], [64 - x, 127 * x, 63 + x])
    for i, ref in enumerate((cross_ref, inward_ref, own_ref)):
        ref[...] = edges[8 * i : 8 * i + 8]


def rest_kernel(plan, tangent_ref, get_ref, *refs):
    chips = plan.chips
    diag_refs, straight_refs, rest_ref = refs[:chips], refs[chips : 2 * chips][::-1], refs[2 * chips]
    z, x, _ = place()
    first = x == 0
    at_face = z == jnp.where(first, plan.inlet, plan.inlet - 1)
    at_end = z == jnp.where(first, 0, plan.pairs - 1)
    get = get_ref[...]
    for c in range(NC):
        straight = get_parts(plan, straight_refs, c)
        diag = get_parts(plan, diag_refs, c)
        slots = unpack2(jnp.where(first, straight, diag), jnp.where(first, diag, straight))
        moved = permuted(get, slots)
        halo = jnp.where(at_face, moved, jnp.where(at_end, 0.0, gathered(plan, slots)))
        down, up = coefficients(c)
        rest_ref[c] = tangent_ref[c] * (jnp.where(first, down, up) * halo)


def last_kernel(plan, partial_ref, rest_ref, tangent_ref, share_ref, *refs):
    cross_ref, inward_ref, own_ref, out_ref = refs
    _, x, _ = place()
    half = plan.rows // 2
    edges = [get_edge(plan, share_ref, 0), cross_ref[...], inward_ref[...], own_ref[...]]
    ghosts = edges_at(
        jnp.concatenate(edges, axis=0), [63 + x, 127 * x, 127 * (1 - x), 64 - x]
    )
    for c in range(NC):
        ghost = ghosts[:, c * LANES : (c + 1) * LANES]
        share = share_ref[c * half : (c + 1) * half]
        rest = rest_ref[c] + tangent_ref[c] * (SPREADING[c] * ghost)
        out_ref[c] = pairing(plan, partial_ref[c], share, x) + rest


def call(kernel, outs, *args, flops=None):
    whole = pl.BlockSpec(memory_space=pltpu.VMEM)
    return pl.pallas_call(
        kernel,
        out_shape=[jax.ShapeDtypeStruct(shape, dtype) for shape, dtype in outs],
        in_specs=[whole] * len(args),
        out_specs=[whole] * len(outs),
        compiler_params=pltpu.CompilerParams(vmem_limit_bytes=32 * 2**20),
        cost_estimate=flops
        and pl.CostEstimate(flops=flops, bytes_accessed=0, transcendentals=0),
    )(*args)


def solution(mesh):
    def local(checkpoint, adjoint, line_inverse, row_source):
        rows = checkpoint.shape[1]
        plan = Plan(mesh, rows, line_inverse.shape[1])
        chips = plan.chips

        def run(kernel, outs, *args, flops=None):
            return call(lambda *refs: kernel(plan, *refs), outs, *args, flops=flops)

        def send(part, moves):
            return lax.ppermute(part, AXES, moves)

        def share(edges):
            return ((NC * rows // 2 + edges * plan.edge_rows, LANES), f32)

        full = ((NC, rows, LANES), f32)
        half = ((NC, rows // 2, LANES), f32)
        edge = ((8, rows), f32)
        parts = ((2, chips, NC, plan.part_pad, LANES), f32)
        put_shape, get_shape = ((plan.slots, rows), bf16), ((rows, plan.slots), bf16)
        checkpoint = checkpoint.reshape(full[0])
        adjoint = adjoint.reshape(full[0])
        inverse = line_inverse.reshape(line_inverse.shape[1:])
        source = row_source.reshape(plan.span, rows)
        source = jnp.pad(source, ((0, -plan.span % 8), (0, 0)), constant_values=-1)

        (mine,) = call(pack_kernel, [half], checkpoint)
        state_got = send(mine, plan.swap_x)
        outward, inward, partner, own = run(edge_kernel, [edge] * 4, checkpoint)
        outward_got = send(outward, plan.outward)
        inward_got = send(inward, plan.inward)
        (carried,) = run(carried_kernel, [full], adjoint, inverse)
        put, get = run(slot_kernel, [put_shape, get_shape], source)
        (mine,) = run(share_kernel, [share(2)], carried, partner, inward_got, outward_got)
        share_got = send(mine, plan.swap_x)
        flux, face, *near = run(
            first_kernel,
            [full, parts] + [half] * len(plan.swap_z),
            *(checkpoint, state_got, put),
        )
        crossed = send(face[1], plan.swap_core)
        near_got = [send(part, moves) for part, moves in zip(near, plan.swap_z)]
        face_got = [
            send(jnp.stack([face[0, t], crossed[t]]), plan.swap_face[t]) for t in range(chips)
        ]
        base, pair, tangent, pair_tangent = run(
            local_kernel,
            [full] * 4,
            *(checkpoint, state_got, flux, carried, share_got, outward_got, own),
        )
        core, partial, mine, straight, diag, weighted = run(
            second_kernel,
            [(parts[0][1:], f32), full, share(1), parts, parts, full],
            *(base, pair, pair_tangent, get, put, *face_got[::-1], *near_got),
        )
        crossed = send(core, plan.swap_core)
        cross, inward, own = run(edge2_kernel, [edge] * 3, weighted)
        share_got = send(mine, plan.swap_x)
        z, x, _ = place()
        turned = jnp.logical_xor(x == 0, z == plan.inlet)
        at_face = jnp.logical_or(z == plan.inlet, z == plan.inlet - 1)

        def halo(part, moves, by_face):
            other = jnp.where(by_face, crossed, part[1])
            return [send(jnp.stack([part[0, t], other[t]]), moves[t]) for t in range(chips)]

        straight_got = halo(straight, plan.straight, jnp.logical_and(at_face, turned))
        diag_got = halo(diag, plan.diag, jnp.logical_and(at_face, jnp.logical_not(turned)))
        (cross, inward), _ = lax.optimization_barrier(((cross, inward), diag_got[0]))
        cross_got = send(cross, plan.cross)
        inward_got = send(inward, plan.inward)
        (rest,) = run(rest_kernel, [full], tangent, get, *diag_got, *straight_got[::-1])
        (out,) = run(
            last_kernel,
            [full],
            *(partial, rest, tangent, share_got, cross_got, inward_got, own),
        )
        return out.reshape(NC, rows, 1, LANES)

    return jax.shard_map(
        local,
        mesh=mesh,
        in_specs=(
            P(None, None, "stream", "span"),
            P(None, None, "stream", "span"),
            P("stream", None, None, None),
            P(),
        ),
        out_specs=P(None, None, "stream", "span"),
        check_vma=False,
    )
```
